32 devices in a mesh: fsdp: 4 (over z), ctx: 2 (over y), tp: 4 (over x, core).
Axes of the slice: x: 2, y: 2, z: 4, core: 2. Of those that a mesh axis runs over, the one named last changes fastest.
Arguments:
- tokens: bfloat16 [16, 1024, 1024], P(('fsdp', 'tp'), 'ctx'), may hold values from -6 to 6
- routes: int32 [16, 1024, 8], P('fsdp', 'ctx'), may hold values from 0 to 31, all different within a row; in each aligned block of 512 rows (0 to 511, 512 to 1023, ..., all dimensions but the last counted through in order) at most 192 rows name the same one
- cotangent: bfloat16 [16, 1024, 1024], P(('fsdp', 'tp'), 'ctx'), may hold values from -6 to 6
- norm_gains: bfloat16 [2, 1024], P(None, ('fsdp', 'ctx', 'tp')), may hold values from 0.25 to 1.75
- query_key_value: bfloat16 [2048, 1024], P(('fsdp', 'ctx', 'tp')), may hold values from -0.25 to 0.25
- attn_output: bfloat16 [1024, 1024], P(('fsdp', 'ctx', 'tp')), may hold values from -0.75 to 0.75
- router_weight: bfloat16 [32, 1024], P(None, ('fsdp', 'ctx', 'tp')), may hold values from -0.09375 to 0.09375
- expert_in: bfloat16 [32, 2, 1024, 512], P(None, None, ('fsdp', 'ctx'), 'tp'), may hold values from -0.1875 to 0.1875
- expert_out: bfloat16 [32, 1024, 512], P(None, ('fsdp', 'ctx'), 'tp'), may hold values from -1 to 1
Outputs:
- output: bfloat16 [16, 1024, 1024], P(('fsdp', 'tp'), 'ctx')
- input_grad: float32 [16, 1024, 1024], P(('fsdp', 'tp'), 'ctx')
- grad_norm_gains: float32 [2, 1024], P(None, ('fsdp', 'ctx', 'tp'))
- grad_query_key_value: float32 [2048, 1024], P(('fsdp', 'ctx', 'tp'))
- grad_attn_output: float32 [1024, 1024], P(('fsdp', 'ctx', 'tp'))
- grad_router_weight: float32 [32, 1024], P(None, ('fsdp', 'ctx', 'tp'))
- grad_expert_in: float32 [32, 2, 1024, 512], P(None, None, ('fsdp', 'ctx'), 'tp')
- grad_expert_out: float32 [32, 1024, 512], P(None, ('fsdp', 'ctx'), 'tp')
The draws below stay inside these ranges and needn't reach their ends.
Inputs may be any that keep to these rules, and one draw needn't show every extreme that they name: `routes`: each row names 8 different experts. In each aligned block of 512 rows (one sequence's positions on one index of ctx), no expert is named by more than 192 rows, a bound that some block reaches.
All inputs are finite; a program needn't handle non-finite values.
Results may differ from the reference program's by a relative error of at most 0.014.
The reference program's roundings to bfloat16 on the way count: a program that leaves them out, or rounds other values in their place, can miss the bound.
Values may be sent and summed in bfloat16 or wider, within the bound.
No kernel may reach another device: no remote copies, remote signals or barrier semaphores. Data moves between devices by JAX's collectives and lax.ppermute only.
A program may use at most 320 MiB of HBM per device.

```python
import math
import jax
import jax.numpy as jnp
import numpy as np
from jax import lax

D = 1024
HEADS = 16
KV_HEADS = 8
HEAD = 64
EXPERTS = 32
TOP = 8
FF = 512
LEN = 1024
QKV = 2048
POS = 512
SEQS = 16
MOST = 192


def block_scale(own_key, extent, split, smallest, largest):
    factor_of, own = 1.0, jax.random.fold_in(own_key, 6)
    for dim, blocks in split:
        heights = jnp.exp(jax.random.uniform(jax.random.fold_in(own, dim), (blocks,), jnp.float32, smallest / len(split), largest / len(split)))
        factor_of = factor_of * jnp.repeat(heights, extent[dim] // blocks).reshape([-1 if axis == dim else 1 for axis in range(len(extent))])
    return factor_of


def routed_block(stream_key, own, number, rows, amount, top, bound, slope):
    order = jax.random.permutation(stream_key, amount)
    heavy_load, ordinary = shares(amount, rows * top, bound, slope, True), shares(amount, rows * top, bound, slope, False)
    places = jnp.arange(amount)

    def named(tallies, turn):
        used = int((tallies > 0).sum())
        fixed = max(1, used // 4)
        moved = fixed + (places - fixed + turn * (used - fixed)) % max(1, amount - fixed)
        return jnp.zeros((amount,), jnp.int32).at[order[jnp.where(places < fixed, places, moved)]].set(jnp.asarray(tallies, jnp.int32))

    tallies = jnp.where(number % 4 == 0, named(heavy_load, number // 4), named(ordinary, number - number // 4 - 1))
    mixed = jax.random.permutation(jax.random.fold_in(own, 3), amount)
    giver, receiver = mixed[0:amount // 2 * 2:2], mixed[1:amount // 2 * 2:2]
    margin = jnp.minimum(tallies[giver] - 1, bound - tallies[receiver]) // 2
    margin = jnp.where((giver == order[0]) | (receiver == order[0]) | (tallies[receiver] == 0), 0, jnp.maximum(margin, 0))
    moved = jax.random.randint(jax.random.fold_in(own, 4), (amount // 2,), 0, 1 << 20) % (margin + 1)
    tallies = tallies.at[giver].add(-moved).at[receiver].add(moved)
    items = jnp.searchsorted(jnp.cumsum(tallies), jnp.arange(rows * top), side="right").astype(jnp.int32)
    grid = items.reshape(top, rows).T
    grid = grid[jax.random.permutation(jax.random.fold_in(own, 1), rows)]
    turn = jax.random.randint(jax.random.fold_in(own, 2), (rows, 1), 0, top)
    return jnp.take_along_axis(grid, (jnp.arange(top)[None, :] + turn) % top, axis=1)


def shares(count, total, bound, slope, full):
    portions = [(1 << 20) // math.isqrt(standing ** slope) + 1 for standing in range(1, count + 1)]
    largest = bound if full else min(bound, max(-(-total // count), total * portions[0] // sum(portions)))
    least = 1 if total - largest >= count - 1 else 0
    given, surplus = [largest] + [least] * (count - 1), total - largest - least * (count - 1)
    while surplus > 0:
        candidates = [i for i in range(1, count) if given[i] < largest] or [i for i in range(1, count) if given[i] < bound]
        pool, budget = sum([portions[i] for i in candidates]), surplus
        for i in candidates:
            more = min(bound - given[i], max(1, budget * portions[i] // pool), surplus)
            given[i] = given[i] + more
            surplus = surplus - more
    return np.array(given)


def gaussian(own_key, dims, width, most, shards=(), kind=jnp.bfloat16):
    entries = width * jax.random.normal(own_key, dims, jnp.float32)
    if shards:
        entries = entries * block_scale(own_key, dims, shards, -0.22, 0.18)
    return jnp.clip(entries, -most, most).astype(kind)


def setup_inputs(seed: int = 0) -> dict:
    keys = jax.random.split(jax.random.key(seed), 10)
    tokens = gaussian(keys[0], (SEQS, LEN, D), 1.0, 6.0, ((0, 16), (1, 2)))
    routes_keys = jax.random.split(jax.random.fold_in(keys[1], 1), SEQS * LEN // POS)
    routes_turns = jax.random.permutation(jax.random.fold_in(keys[1], 3), SEQS * LEN // POS)
    routes = jax.vmap(lambda own, number: routed_block(jax.random.fold_in(keys[1], 2), own, number, POS, EXPERTS, TOP, MOST, 2))(routes_keys, routes_turns).reshape((SEQS, LEN, TOP))
    cotangent = gaussian(keys[2], (SEQS, LEN, D), 1.0, 6.0, ((0, 16), (1, 2)))
    norm_gains = jnp.clip(1.0 + 0.15 * jax.random.normal(keys[3], (2, D), jnp.float32), 0.25, 1.75).astype(jnp.bfloat16)
    query_key_value = gaussian(keys[4], (QKV, D), (D // 2) ** -0.5, 0.25, ((0, 32),))
    attn_output = gaussian(keys[5], (D, HEADS * HEAD), (HEADS * HEAD // 16) ** -0.5, 0.75, ((0, 32),))
    router_weight = gaussian(keys[6], (EXPERTS, D), (4 * D) ** -0.5, 0.09375, ((1, 32),))
    expert_in = gaussian(keys[7], (EXPERTS, 2, D, FF), D ** -0.5, 0.1875, ((2, 8), (3, 4)))
    expert_out = gaussian(keys[8], (EXPERTS, D, FF), (FF // 16) ** -0.5, 1.0, ((1, 8), (2, 4)))
    return dict(tokens=tokens, routes=routes, cotangent=cotangent, norm_gains=norm_gains, query_key_value=query_key_value, attn_output=attn_output, router_weight=router_weight, expert_in=expert_in, expert_out=expert_out)


EPS = 1e-06
NEG = -1e+30
HIGH = lax.Precision.HIGHEST

@jax.custom_vjp
def low(v):
    return lax.optimization_barrier(v.astype(jnp.bfloat16)).astype(jnp.float32)

@jax.custom_vjp
def low_back(v):
    return v

def low_keep(v):
    return (low(v), None)

def low_pass(kept, grad):
    return (grad,)

def back_keep(v):
    return (v, None)

def back_low(kept, grad):
    return (low(grad),)
low.defvjp(low_keep, low_pass)
low_back.defvjp(back_keep, back_low)

def angle_tables(positions, head_size):
    half_size = head_size // 2
    inverse = 10000.0 ** (-jnp.arange(half_size, dtype=jnp.float32) * 2.0 / head_size)
    angles = positions.astype(jnp.float32)[:, None] * inverse[None, :]
    return (jnp.cos(angles), jnp.sin(angles))

def rotary(values, cosine_table, sine_table):
    half_size = values.shape[-1] // 2
    former = values[..., :half_size]
    latter = values[..., half_size:]
    return jnp.concatenate([former * cosine_table - latter * sine_table, latter * cosine_table + former * sine_table], axis=-1)

def attend(pieces):
    queries, key_rows, value_rows = pieces
    score_scale = HEAD ** (-0.5)
    scores = low_back(jnp.einsum('qgjd,kgd->gjqk', queries, key_rows, precision=HIGH) * score_scale)
    visible = jnp.arange(LEN)[:, None] >= jnp.arange(LEN)[None, :]
    scores = jnp.where(visible, scores, NEG)
    weights = low(jax.nn.softmax(scores, axis=-1))
    return jnp.einsum('gjqk,kgd->qgjd', weights, value_rows, precision=HIGH)

def slot_table(route_rows, segments):
    per_segment = route_rows.reshape(segments, POS * TOP)
    marking = (per_segment[:, :, None] == jnp.arange(EXPERTS, dtype=jnp.int32)[None, None, :]).astype(jnp.int32)
    ranking = lax.optimization_barrier(jnp.sum((jnp.cumsum(marking, axis=1) - 1) * marking, axis=2))
    slot_ids = per_segment * (segments * MOST) + jnp.arange(segments, dtype=jnp.int32)[:, None] * MOST + ranking
    slot_ids = slot_ids.reshape(-1)
    capacity = EXPERTS * segments * MOST
    source = jnp.zeros((capacity,), jnp.int32).at[slot_ids].set(jnp.arange(slot_ids.shape[0], dtype=jnp.int32))
    filled = jnp.zeros((capacity,), jnp.float32).at[slot_ids].set(1.0)
    return (source, filled)

def forward(params, inputs, route_group):
    norm_gains, query_key_value, attn_output, router_weight, expert_in, expert_out = params
    seq_count = inputs.shape[0]
    row_count = seq_count * LEN
    flat_rows = inputs.reshape(row_count, D)
    normed_first = flat_rows * lax.rsqrt(lax.optimization_barrier(jnp.mean(flat_rows * flat_rows, axis=1, keepdims=True)) + EPS)
    first_low = low(normed_first * norm_gains[0])
    projected = low_back(jnp.dot(first_low, query_key_value.T, precision=HIGH)).reshape(seq_count, LEN, KV_HEADS, 4, HEAD)
    cosine_table, sine_table = angle_tables(jnp.arange(LEN, dtype=jnp.int32), HEAD)
    cosine_rows = cosine_table[None, :, None, None, :]
    sine_rows = sine_table[None, :, None, None, :]
    turned = jnp.concatenate([rotary(projected[:, :, :, :3], cosine_rows, sine_rows), projected[:, :, :, 3:]], axis=3)
    heads = low(low_back(turned))
    attended = lax.map(jax.checkpoint(attend), (heads[:, :, :, :2], heads[:, :, :, 2], heads[:, :, :, 3]))
    merged = low(low_back(attended.reshape(row_count, HEADS * HEAD)))
    hidden = flat_rows + low_back(jnp.dot(merged, attn_output.T, precision=HIGH))
    normed_second = hidden * lax.rsqrt(lax.optimization_barrier(jnp.mean(hidden * hidden, axis=1, keepdims=True)) + EPS)
    second = low(normed_second * norm_gains[1])
    chances = jax.nn.softmax(jnp.dot(second, router_weight.T, precision=HIGH), axis=-1)
    route_rows = route_group.reshape(row_count, TOP)
    gate_values = jnp.take_along_axis(chances, route_rows, axis=1)
    segments = row_count // POS
    source, filled = slot_table(route_rows, segments)
    slot_rows = segments * MOST
    token_ids = (source // TOP).reshape(EXPERTS, slot_rows)
    slot_gates = (gate_values.reshape(-1)[source] * filled).reshape(EXPERTS, slot_rows)

    def expert_apply(pieces):
        ids_block, weight_in, weight_out = pieces
        rows_in = second[ids_block]
        pre_gate = low_back(jnp.dot(rows_in, weight_in[0], precision=HIGH))
        pre_up = low_back(jnp.dot(rows_in, weight_in[1], precision=HIGH))
        hidden_rows = low(jax.nn.silu(pre_gate) * pre_up)
        return low_back(jnp.dot(hidden_rows, weight_out.T, precision=HIGH))
    expert_rows = lax.map(jax.checkpoint(expert_apply), (token_ids, expert_in, expert_out))
    combined = jnp.zeros((row_count, D), jnp.float32).at[token_ids.reshape(-1)].add((expert_rows * slot_gates[:, :, None]).reshape(-1, D))
    return (hidden + low_back(combined)).reshape(inputs.shape)

def reference(tokens, routes, cotangent, norm_gains, query_key_value, attn_output, router_weight, expert_in, expert_out):
    params = (norm_gains.astype(jnp.float32), query_key_value.astype(jnp.float32), attn_output.astype(jnp.float32), router_weight.astype(jnp.float32), expert_in.astype(jnp.float32), expert_out.astype(jnp.float32))
    group_size = math.gcd(SEQS, max(1, 4096 // LEN))
    group_count = SEQS // group_size
    inputs = tokens.astype(jnp.float32).reshape(group_count, group_size, LEN, D)
    route_groups = routes.reshape(group_count, group_size, LEN, TOP)
    cot_groups = cotangent.astype(jnp.float32).reshape(group_count, group_size, LEN, D)

    def group_step(running, pieces):
        group_in, group_routes, group_cot = pieces
        result, pullback = jax.vjp(lambda weights, values: forward(weights, values, group_routes), params, group_in)
        weight_grads, input_grads = pullback(group_cot)
        running = jax.tree.map(jnp.add, running, weight_grads)
        return (running, (result.astype(jnp.bfloat16), input_grads))
    initial = jax.tree.map(jnp.zeros_like, params)
    totals, (results, input_grads) = lax.scan(group_step, initial, (inputs, route_groups, cot_groups))
    return (results.reshape(SEQS, LEN, D), input_grads.reshape(SEQS, LEN, D), totals[0], totals[1], totals[2], totals[3], totals[4], totals[5])
```

```python
import functools

import jax
import jax.numpy as jnp
from jax import lax
from jax.experimental import pallas as pl
from jax.experimental.pallas import tpu as pltpu
from jax.sharding import PartitionSpec as P

HEADS = 16
KV_HEADS = 8
HEAD = 64
EXPERTS = 32
TOP = 8


EPS = 1e-06
NEG = -1e30
HIGH = lax.Precision.HIGHEST
ALL_AXES = ("fsdp", "ctx", "tp")
CHUNKS = 4
TILE = 512
LANES = 128


def times_transposed(left_side, right_side):
    return lax.dot_general(
        left_side, right_side, (((1,), (1,)), ((), ())), preferred_element_type=jnp.float32
    )


def transposed_times(left_side, right_side):
    return lax.dot_general(
        left_side, right_side, (((0,), (0,)), ((), ())), preferred_element_type=jnp.float32
    )


def angle_tables(positions, head_size):
    half_size = head_size // 2
    inverse = 10000.0 ** (-jnp.arange(half_size, dtype=jnp.float32) * 2.0 / head_size)
    angles = positions.astype(jnp.float32)[:, None] * inverse[None, :]
    return (jnp.cos(angles), jnp.sin(angles))


def rotary(values, cosine_table, sine_table):
    half_size = values.shape[-1] // 2
    former = values[..., :half_size]
    latter = values[..., half_size:]
    return jnp.concatenate(
        [former * cosine_table - latter * sine_table, latter * cosine_table + former * sine_table],
        axis=-1,
    )


def rotary_back(gradient, cosine_table, sine_table):
    half_size = gradient.shape[-1] // 2
    former = gradient[..., :half_size]
    latter = gradient[..., half_size:]
    return jnp.concatenate(
        [former * cosine_table + latter * sine_table, latter * cosine_table - former * sine_table],
        axis=-1,
    )


def rms_back(grad_normed, normed, inverse, gain_row):
    scaled_grad = grad_normed * gain_row
    return inverse * (scaled_grad - normed * jnp.mean(scaled_grad * normed, axis=1, keepdims=True))


def dot_nn(left_side, right_side):
    return lax.dot_general(
        left_side, right_side, (((1,), (0,)), ((), ())), preferred_element_type=jnp.float32
    )


def pack_rows(pieces, width):
    flat = jnp.concatenate([piece.reshape(-1) for piece in pieces])
    rows = -(-flat.shape[0] // (16 * width)) * 16
    return jnp.pad(flat, (0, rows * width - flat.shape[0])).reshape(rows, width)


def expert_kernel(first, steps, base_expert, extra, places_ref, *refs):
    count = len(steps)
    weight_refs, refs = refs[:count], refs[count:]
    rows_ref, rows_turned_ref, grad_ref, grad_turned_ref, gate_ref = refs[:5]
    refs = refs[5:]
    if not first:
        moe_in_ref, back_in_ref = refs[:2]
        refs = refs[2:]
    refs = refs[extra:]
    moe_ref, back_ref, choice_ref = refs[:3]
    out_refs, refs = refs[3 : 3 + count], refs[3 + count + extra :]
    moe, back, weight_in, weight_out, hidden_rows, grad_hidden, stage, semaphores = refs
    pair = pl.program_id(0)
    token_count = rows_ref.shape[0]
    units = weight_refs[0].shape[-1]
    depth = weight_refs[0].shape[-2]
    width = 2 * units

    last = pl.num_programs(0) - 1
    tiles = token_count // TILE

    def moves(tile, inward):
        rows = pl.ds(pl.multiple_of(tile * TILE, TILE), TILE)
        if inward:
            return (
                pltpu.make_async_copy(moe_in_ref.at[rows], moe.at[rows], semaphores.at[0, tile]),
                pltpu.make_async_copy(back_in_ref.at[rows], back.at[rows], semaphores.at[1, tile]),
            )
        return (
            pltpu.make_async_copy(moe.at[rows], moe_ref.at[rows], semaphores.at[2, tile]),
            pltpu.make_async_copy(back.at[rows], back_ref.at[rows], semaphores.at[3, tile]),
        )

    if not first:

        @pl.when(pair == 0)
        def _():
            for tile in range(tiles):
                for move in moves(tile, True):
                    move.start()

    @pl.when(pair == 0)
    def _():
        choice_ref[...] = jnp.zeros_like(choice_ref)
        if first:
            moe[...] = jnp.zeros_like(moe)
            back[...] = jnp.zeros_like(back)

    def place(number, block):
        return pl.ds(
            pl.multiple_of(places_ref[number] + block * steps[number], depth), depth
        )

    for number, ref in enumerate(weight_refs):
        for block in range(ref.shape[0]):
            where = place(number, block)
            for which in range(2):
                columns = slice(which * units, (which + 1) * units)
                weight_in[where, columns] = ref[block, which, 0]
                weight_in[where, width + which * units : width + (which + 1) * units] = ref[
                    block, which, 1
                ]
                weight_out[where, columns] = ref[block, which, 2]

    expert = base_expert + 2 * pair

    def tile_step(tile, carry):
        rows = pl.ds(pl.multiple_of(tile * TILE, TILE), TILE)
        both = dot_nn(rows_ref[rows, :], weight_in[...])
        probe = dot_nn(grad_ref[rows, :], weight_out[...])
        gates = gate_ref[rows, :]
        lane = lax.broadcasted_iota(jnp.int32, gates.shape, 1)
        pre_gate = both[:, :width]
        pre_up = both[:, width:]
        gate = jnp.concatenate(
            [
                jnp.broadcast_to(
                    jnp.sum(
                        jnp.where(lane == expert + which, gates, 0.0), axis=1, keepdims=True
                    ),
                    (TILE, units),
                )
                for which in range(2)
            ],
            axis=1,
        )
        sigmoid_gate = 1.0 / (1.0 + jnp.exp(-pre_gate))
        swish_gate = pre_gate * sigmoid_gate
        hidden = (swish_gate * pre_up).astype(jnp.bfloat16).astype(jnp.float32)
        gated = (hidden * gate).astype(jnp.bfloat16)
        product = probe * hidden
        choice = choice_ref[rows, :]
        for which in range(2):
            total = jnp.sum(
                product[:, which * units : (which + 1) * units], axis=1, keepdims=True
            )
            choice = jnp.where(lane == expert + which, total, choice)
        choice_ref[rows, :] = choice
        scaled = probe * gate
        grad_gate = (
            scaled * pre_up * sigmoid_gate * (1.0 + pre_gate * (1.0 - sigmoid_gate))
        ).astype(jnp.bfloat16)
        grad_up = (scaled * swish_gate).astype(jnp.bfloat16)
        hidden_rows[rows, :] = gated
        grad_hidden[rows, :width] = grad_gate
        grad_hidden[rows, width:] = grad_up
        if not first:

            @pl.when(pair == 0)
            def _():
                for move in moves(tile, True):
                    move.wait()

        moe[rows, :] += times_transposed(gated, weight_out[...])
        back[rows, :] += times_transposed(
            jnp.concatenate([grad_gate, grad_up], axis=1), weight_in[...]
        )

        @pl.when(pair == last)
        def _():
            for move in moves(tile, False):
                move.start()

        return carry

    lax.fori_loop(0, tiles, tile_step, 0)

    slab = 256

    def weight_step(tile, carry):
        rows = pl.ds(pl.multiple_of(tile * slab, slab), slab)
        stage[rows, : 2 * width] = dot_nn(rows_turned_ref[rows, :], grad_hidden[...]).astype(
            jnp.bfloat16
        )
        stage[rows, 2 * width :] = dot_nn(grad_turned_ref[rows, :], hidden_rows[...]).astype(
            jnp.bfloat16
        )
        return carry

    lax.fori_loop(0, rows_turned_ref.shape[0] // slab, weight_step, 0)

    for number, ref in enumerate(out_refs):
        for block in range(ref.shape[0]):
            where = place(number, block)
            for which in range(2):
                for kind in range(3):
                    start = kind * width + which * units
                    ref[block, which, kind] = stage[where, start : start + units]

    @pl.when(pair == last)
    def _():
        for tile in range(tiles):
            for move in moves(tile, False):
                move.wait()


def expert_pass(
    places, steps, weights, rows, rows_turned, grads, grads_turned, gates, totals, base_expert, earlier=()
):
    first = totals is None
    token_count, model_width = rows.shape
    experts, _, depth, units = weights[0].shape[1:]

    def whole(array):
        return pl.BlockSpec(
            array.shape, lambda *_: (0,) * array.ndim, pipeline_mode=pl.Buffered(1)
        )

    weight_specs = [
        pl.BlockSpec((piece.shape[0], 2, 3, depth, units), lambda pair, _: (0, pair, 0, 0, 0))
        for piece in weights
    ]
    operands = [*weights, rows, rows_turned, grads, grads_turned, gates]
    specs = [*weight_specs, *(whole(array) for array in operands[len(weights) :])]
    aliases = {}
    if not first:
        aliases = {1 + len(operands): 0, 2 + len(operands): 1}
        operands += list(totals)
        specs += [pl.BlockSpec(memory_space=pl.ANY)] * 2
    for number, array in enumerate(earlier):
        aliases[1 + len(operands)] = 3 + len(weights) + number
        operands.append(array)
        specs.append(pl.BlockSpec(memory_space=pl.ANY))
    total_shape = jax.ShapeDtypeStruct((token_count, model_width), jnp.float32)
    products = 2 * token_count * model_width * units * experts
    return pl.pallas_call(
        functools.partial(expert_kernel, first, steps, base_expert, len(earlier)),
        grid_spec=pltpu.PrefetchScalarGridSpec(
            num_scalar_prefetch=1,
            grid=(experts // 2,),
            in_specs=specs,
            out_specs=[
                pl.BlockSpec(memory_space=pl.ANY),
                pl.BlockSpec(memory_space=pl.ANY),
                pl.BlockSpec((token_count, LANES), lambda *_: (0, 0)),
                *weight_specs,
                *([pl.BlockSpec(memory_space=pl.ANY)] * len(earlier)),
            ],
            scratch_shapes=[
                pltpu.VMEM((token_count, model_width), jnp.float32),
                pltpu.VMEM((token_count, model_width), jnp.float32),
                pltpu.VMEM((model_width, 4 * units), jnp.bfloat16),
                pltpu.VMEM((model_width, 2 * units), jnp.bfloat16),
                pltpu.VMEM((token_count, 2 * units), jnp.bfloat16),
                pltpu.VMEM((token_count, 4 * units), jnp.bfloat16),
                pltpu.VMEM((model_width, 6 * units), jnp.bfloat16),
                pltpu.SemaphoreType.DMA((4, token_count // TILE)),
            ],
        ),
        out_shape=[
            total_shape,
            total_shape,
            jax.ShapeDtypeStruct((token_count, LANES), jnp.float32),
            *(jax.ShapeDtypeStruct(piece.shape, jnp.bfloat16) for piece in weights),
            *(jax.ShapeDtypeStruct(array.shape, array.dtype) for array in earlier),
        ],
        input_output_aliases=aliases,
        compiler_params=pltpu.CompilerParams(
            dimension_semantics=("arbitrary",), vmem_limit_bytes=60 * 2**20
        ),
        cost_estimate=pl.CostEstimate(
            flops=9 * products,
            bytes_accessed=40 * 2**20,
            transcendentals=token_count * units * experts,
        ),
    )(places, *operands)


def swap_pairs(count, bit):
    return [(index, index ^ bit) for index in range(count)]


def gather_group(rows):
    count = lax.axis_size("tp")
    across = lax.ppermute(rows, "tp", swap_pairs(count, 2))
    beside = lax.ppermute(rows, "tp", swap_pairs(count, 1))
    corner = lax.ppermute(across, "tp", swap_pairs(count, 1))
    return jnp.concatenate([rows, beside, across, corner], axis=0)


def scatter_group(terms):
    count = lax.axis_size("tp")
    parts = terms.reshape(count, -1, terms.shape[-1])
    sent = lax.ppermute(
        parts[1::2].astype(jnp.bfloat16), "tp", swap_pairs(count, 1)
    ).astype(jnp.float32)
    kept = parts[0] + sent[0]
    passed = (parts[2] + sent[1]).astype(jnp.bfloat16)
    return kept + lax.ppermute(passed, "tp", swap_pairs(count, 2)).astype(jnp.float32)


def shifted(count, step):
    return [(index, (index + step) % count) for index in range(count)]


def gather_axis(piece, name):
    count = lax.axis_size(name)
    mine = lax.axis_index(name)
    found = [piece] + [
        lax.ppermute(piece, name, shifted(count, -step)) for step in range(1, count)
    ]
    return lax.dynamic_slice_in_dim(
        jnp.stack(found + found[:-1]), (count - mine) % count, count, axis=0
    )


def gather_bit(piece, bit):
    other = lax.ppermute(piece, "tp", swap_pairs(lax.axis_size("tp"), bit))
    upper = (lax.axis_index("tp") & bit) > 0
    return jnp.where(upper, jnp.stack([other, piece]), jnp.stack([piece, other]))


def gather_dense(piece):
    fsdp_count, context_count = lax.axis_size("fsdp"), lax.axis_size("ctx")
    whole = gather_bit(gather_bit(gather_axis(gather_axis(piece, "fsdp"), "ctx"), 2), 1)
    whole = whole.reshape((2, 2, context_count, fsdp_count) + piece.shape)
    return whole.transpose(3, 2, 1, 0, 4, 5).reshape((-1,) + piece.shape)


def scatter_axis(parts, name):
    count = lax.axis_size(name)
    mine = lax.axis_index(name)
    low = parts.astype(jnp.bfloat16)
    total = lax.dynamic_index_in_dim(parts, mine, 0, keepdims=False).astype(jnp.float32)
    for step in range(1, count):
        sent = lax.dynamic_index_in_dim(low, (mine + step) % count, 0, keepdims=False)
        total = total + lax.ppermute(sent, name, shifted(count, step)).astype(jnp.float32)
    return total


def scatter_bit(parts, bit):
    mine = (lax.axis_index("tp") & bit) // bit
    sent = lax.dynamic_index_in_dim(parts, 1 - mine, 0, keepdims=False).astype(jnp.bfloat16)
    kept = lax.dynamic_index_in_dim(parts, mine, 0, keepdims=False).astype(jnp.float32)
    return kept + lax.ppermute(sent, "tp", swap_pairs(lax.axis_size("tp"), bit)).astype(
        jnp.float32
    )


def scatter_dense(parts):
    fsdp_count, context_count = lax.axis_size("fsdp"), lax.axis_size("ctx")
    parts = parts.reshape((fsdp_count, context_count, 2, 2) + parts.shape[1:])
    parts = parts.transpose(3, 2, 1, 0, 4, 5)
    return scatter_axis(scatter_axis(scatter_bit(scatter_bit(parts, 1), 2), "ctx"), "fsdp")


def hold(*refs):
    pass


def together(*values):
    spec = pl.BlockSpec(memory_space=pl.ANY)
    return pl.pallas_call(
        hold,
        in_specs=[spec] * len(values),
        out_specs=[spec] * len(values),
        out_shape=[jax.ShapeDtypeStruct(value.shape, value.dtype) for value in values],
        input_output_aliases={number: number for number in range(len(values))},
    )(*values)


def after(value, *earlier):
    spec = pl.BlockSpec(memory_space=pl.ANY)
    return pl.pallas_call(
        hold,
        in_specs=[spec] * (1 + len(earlier)),
        out_specs=spec,
        out_shape=jax.ShapeDtypeStruct(value.shape, value.dtype),
        input_output_aliases={0: 0},
    )(value, *earlier)


def per_device(
    tokens,
    routes,
    cotangent,
    norm_gains,
    query_key_value,
    attn_output,
    router_weight,
    expert_in,
    expert_out,
):
    local_seqs, local_positions, model_width = tokens.shape
    context_count = lax.axis_size("ctx")
    length = local_positions * context_count
    row_count = local_seqs * local_positions
    local_groups = KV_HEADS // context_count
    head_size = HEAD
    score_scale = HEAD ** (-0.5)
    capacity = local_positions * 3 // 8
    device_count = context_count * lax.axis_size("fsdp") * lax.axis_size("tp")
    inward_count, output_count = query_key_value.size, attn_output.size
    gain_count, router_count = norm_gains.size, router_weight.size
    packed = lax.all_gather(pack_rows([query_key_value, norm_gains], model_width), ALL_AXES, axis=0)
    packed_later = gather_dense(pack_rows([attn_output, router_weight], model_width))
    inward_rows, output_rows = query_key_value.shape[0], attn_output.shape[0]
    inward_full = packed[:, :inward_rows].reshape(-1, model_width)
    gain_full = (
        packed[:, inward_rows:]
        .reshape(device_count, -1)[:, :gain_count]
        .reshape(device_count, 2, -1)
        .transpose(1, 0, 2)
        .reshape(2, model_width)
    )
    output_full = packed_later[:, :output_rows].reshape(-1, model_width)
    router_full = (
        packed_later[:, output_rows:]
        .reshape(device_count, -1)[:, :router_count]
        .reshape(device_count, EXPERTS, -1)
        .transpose(1, 0, 2)
        .reshape(EXPERTS, model_width)
    )
    paired = context_count == 2
    expert_shards = jnp.concatenate([expert_in, expert_out[:, None]], axis=1)
    shard_depth = expert_in.shape[2]
    chunk_experts = EXPERTS // CHUNKS
    my_context = lax.axis_index("ctx").astype(jnp.int32)
    if paired:
        places = jnp.stack([my_context, 1 - my_context]) * shard_depth
        steps = (2 * shard_depth, 2 * shard_depth)
    else:
        places = jnp.zeros((1,), jnp.int32)
        steps = (shard_depth,)
    expert_pieces = []
    for chunk in range(CHUNKS):
        shard = expert_shards[chunk * chunk_experts : (chunk + 1) * chunk_experts]
        if paired:
            expert_pieces.append([lax.all_gather(shard, "fsdp", axis=0)])
        else:
            expert_pieces.append([lax.all_gather(shard, ("fsdp", "ctx"), axis=0)])
    gain_rows = gain_full.astype(jnp.float32)
    inputs = tokens.astype(jnp.float32).reshape(row_count, model_width)
    inverse_first = lax.rsqrt(jnp.mean(inputs * inputs, axis=1, keepdims=True) + EPS)
    normed_first = inputs * inverse_first
    first_low = (normed_first * gain_rows[0]).astype(jnp.bfloat16)
    projected = times_transposed(first_low, inward_full).reshape(
        local_seqs, local_positions, KV_HEADS, 4, head_size
    )
    positions = lax.axis_index("ctx") * local_positions + jnp.arange(
        local_positions, dtype=jnp.int32
    )
    cosine_table, sine_table = angle_tables(positions, head_size)
    cosine_rows = cosine_table[None, :, None, None, :]
    sine_rows = sine_table[None, :, None, None, :]
    turned = jnp.concatenate(
        [rotary(projected[:, :, :, :3], cosine_rows, sine_rows), projected[:, :, :, 3:]], axis=3
    )
    sent_heads = turned.astype(jnp.bfloat16).reshape(
        local_seqs, local_positions, KV_HEADS, 4 * head_size
    )
    head_rows = lax.all_to_all(sent_heads, "ctx", split_axis=2, concat_axis=1, tiled=True)
    queries = head_rows[..., : 2 * head_size].reshape(
        local_seqs, length, local_groups, 2, head_size
    )
    key_rows = head_rows[..., 2 * head_size : 3 * head_size]
    value_rows = head_rows[..., 3 * head_size :]
    block_rows = min(512, length)
    key_index = jnp.arange(length)
    attended = []
    log_totals = []
    for offset in range(0, length, block_rows):
        limit_row = offset + block_rows
        scores = (
            jnp.einsum(
                "sqgjd,skgd->sgjqk",
                queries[:, offset:limit_row],
                key_rows[:, :limit_row],
                preferred_element_type=jnp.float32,
            )
            * score_scale
        )
        visible = (offset + jnp.arange(block_rows))[:, None] >= key_index[None, :limit_row]
        scores = jnp.where(visible, scores, NEG)
        top_score = jnp.max(scores, axis=-1, keepdims=True)
        exponent = jnp.exp(scores - top_score)
        denominator = jnp.sum(exponent, axis=-1, keepdims=True)
        weights = exponent / denominator
        attended.append(
            jnp.einsum(
                "sgjqk,skgd->sqgjd",
                weights.astype(jnp.bfloat16),
                value_rows[:, :limit_row],
                preferred_element_type=jnp.float32,
            )
        )
        log_totals.append(top_score + jnp.log(denominator))
    head_output = (
        jnp.concatenate(attended, axis=1)
        .astype(jnp.bfloat16)
        .reshape(local_seqs, length, local_groups, 2 * head_size)
    )
    merged = lax.all_to_all(head_output, "ctx", split_axis=1, concat_axis=2, tiled=True).reshape(
        row_count, HEADS * head_size
    )
    hidden = inputs + times_transposed(merged, output_full)
    inverse_second = lax.rsqrt(jnp.mean(hidden * hidden, axis=1, keepdims=True) + EPS)
    normed_second = hidden * inverse_second
    second_low = (normed_second * gain_rows[1]).astype(jnp.bfloat16)
    group_rows = gather_group(second_low)
    group_grads = gather_group(cotangent.reshape(row_count, model_width))
    group_count = group_rows.shape[0]
    chances = jax.nn.softmax(times_transposed(group_rows, router_full), axis=-1)
    group_order = jnp.bitwise_xor(
        jnp.arange(lax.axis_size("tp"), dtype=jnp.int32), lax.axis_index("tp").astype(jnp.int32)
    )
    route_rows = jnp.take(
        routes.reshape(lax.axis_size("tp"), row_count, TOP), group_order, axis=0
    ).reshape(group_count, TOP)
    chosen_any = jnp.sum(
        (route_rows[:, :, None] == jnp.arange(EXPERTS, dtype=jnp.int32)[None, None, :]).astype(
            jnp.float32
        ),
        axis=1,
    )
    gates = jnp.pad(chances * chosen_any, ((0, 0), (0, LANES - EXPERTS)))
    group_turned = group_rows.T
    grads_turned = group_grads.T
    totals = None
    choice_total = None
    chunk_sums = []
    own_sums = []
    arrivals = []
    marks = []

    def fetch(chunk):
        near = expert_pieces[chunk][0]
        if chunk > 1:
            near = after(near, marks[chunk - 2])
            expert_pieces[chunk][0] = near
        expert_pieces[chunk].append(lax.ppermute(near, "ctx", swap_pairs(2, 1)))

    if paired:
        fetch(0)
    for chunk in range(CHUNKS):
        if paired:
            if chunk + 1 < CHUNKS:
                fetch(chunk + 1)
        moe_total, back_total, choice, *grad_pieces = expert_pass(
            places,
            steps,
            expert_pieces[chunk],
            group_rows,
            group_turned,
            group_grads,
            grads_turned,
            gates,
            totals,
            chunk * chunk_experts,
            arrivals[chunk - 2 : chunk - 1] if chunk > 1 else (),
        )
        totals = (moe_total, back_total)
        marks.append(choice)
        choice_total = choice if choice_total is None else choice_total + choice
        if paired:
            if chunk > 1:
                arrivals[chunk - 2] = grad_pieces[2]
            own_sums.append(grad_pieces[0])
            arrivals.append(lax.ppermute(grad_pieces[1], "ctx", swap_pairs(2, 1)))
        else:
            chunk_sums.append(
                lax.psum_scatter(grad_pieces[0], ("fsdp", "ctx"), scatter_dimension=0)
            )
    grad_chances = choice_total[:, :EXPERTS] * chosen_any
    grad_logits = chances * (grad_chances - jnp.sum(grad_chances * chances, axis=-1, keepdims=True))
    router_rows = router_full.astype(jnp.float32)
    grad_router = jnp.dot(grad_logits.T, group_rows.astype(jnp.float32), precision=HIGH)
    back_group = totals[1] + jnp.dot(grad_logits, router_rows, precision=HIGH)
    grad_second = scatter_group(back_group)
    moe_rows = scatter_group(totals[0])
    output = (hidden + moe_rows).astype(jnp.bfloat16).reshape(tokens.shape)
    grad_gain_second = jnp.sum(grad_second * normed_second, axis=0)
    grad_hidden = cotangent.astype(jnp.float32).reshape(row_count, model_width) + rms_back(
        grad_second, normed_second, inverse_second, gain_rows[1]
    )
    grad_attn = grad_hidden.astype(jnp.bfloat16)
    grad_output_weight = transposed_times(grad_attn, merged)
    grad_merged = (
        jnp.dot(grad_attn, output_full, preferred_element_type=jnp.float32)
        .astype(jnp.bfloat16)
        .reshape(local_seqs, local_positions, KV_HEADS, 2 * head_size)
    )
    grad_heads = lax.all_to_all(grad_merged, "ctx", split_axis=2, concat_axis=1, tiled=True)
    if paired:
        grad_heads, arrivals[-2] = together(grad_heads, arrivals[-2])
    grad_keys = jnp.zeros((local_seqs, length, local_groups, head_size), jnp.float32)
    grad_values = jnp.zeros((local_seqs, length, local_groups, head_size), jnp.float32)
    grad_query_blocks = []
    for offset, log_total in zip(range(0, length, block_rows), log_totals):
        limit_row = offset + block_rows
        query_block = queries[:, offset:limit_row]
        key_part = key_rows[:, :limit_row]
        value_part = value_rows[:, :limit_row]
        scores = (
            jnp.einsum(
                "sqgjd,skgd->sgjqk", query_block, key_part, preferred_element_type=jnp.float32
            )
            * score_scale
        )
        visible = (offset + jnp.arange(block_rows))[:, None] >= key_index[None, :limit_row]
        scores = jnp.where(visible, scores, NEG)
        weights = jnp.exp(scores - log_total)
        grad_block = grad_heads[:, offset:limit_row].reshape(
            local_seqs, block_rows, local_groups, 2, head_size
        )
        grad_values = grad_values.at[:, :limit_row].add(
            jnp.einsum(
                "sgjqk,sqgjd->skgd",
                weights.astype(jnp.bfloat16),
                grad_block,
                preferred_element_type=jnp.float32,
            )
        )
        grad_weights = jnp.einsum(
            "sqgjd,skgd->sgjqk", grad_block, value_part, preferred_element_type=jnp.float32
        )
        grad_scores = (
            weights * (grad_weights - jnp.sum(weights * grad_weights, axis=-1, keepdims=True))
        ).astype(jnp.bfloat16)
        grad_query_blocks.append(
            jnp.einsum(
                "sgjqk,skgd->sqgjd", grad_scores, key_part, preferred_element_type=jnp.float32
            )
            * score_scale
        )
        grad_keys = grad_keys.at[:, :limit_row].add(
            jnp.einsum(
                "sgjqk,sqgjd->skgd", grad_scores, query_block, preferred_element_type=jnp.float32
            )
            * score_scale
        )
    grad_queries = jnp.concatenate(grad_query_blocks, axis=1).reshape(
        local_seqs, length, local_groups, 2 * head_size
    )
    grad_head_rows = jnp.concatenate([grad_queries, grad_keys, grad_values], axis=-1).astype(
        jnp.bfloat16
    )
    if paired:
        grad_head_rows, arrivals[-1] = together(grad_head_rows, arrivals[-1])
        for own, arrived in zip(own_sums, arrivals):
            joined = (own.astype(jnp.float32) + arrived.astype(jnp.float32)).astype(jnp.bfloat16)
            chunk_sums.append(lax.psum_scatter(joined, "fsdp", scatter_dimension=0))
    grad_turned = (
        lax.all_to_all(grad_head_rows, "ctx", split_axis=1, concat_axis=2, tiled=True)
        .astype(jnp.float32)
        .reshape(local_seqs, local_positions, KV_HEADS, 4, head_size)
    )
    grad_projected = (
        jnp.concatenate(
            [
                rotary_back(grad_turned[:, :, :, :3], cosine_rows, sine_rows),
                grad_turned[:, :, :, 3:],
            ],
            axis=3,
        )
        .astype(jnp.bfloat16)
        .reshape(row_count, -1)
    )
    grad_inward = transposed_times(grad_projected, first_low)
    grad_first = jnp.dot(grad_projected, inward_full, preferred_element_type=jnp.float32)
    grad_gain_first = jnp.sum(grad_first * normed_first, axis=0)
    grad_inputs = grad_hidden + rms_back(grad_first, normed_first, inverse_first, gain_rows[0])

    def by_device(array, axis):
        parts = array.reshape(
            array.shape[:axis] + (device_count, -1) + array.shape[axis + 1 :]
        )
        return jnp.moveaxis(parts, axis, 0).reshape(device_count, -1)

    def sum_dense(terms):
        flat = jnp.concatenate(terms, axis=1)
        rows = -(-flat.shape[1] // (8 * model_width)) * 8
        flat = jnp.pad(flat, ((0, 0), (0, rows * model_width - flat.shape[1])))
        return scatter_dense(flat.reshape(device_count, rows, model_width)).reshape(-1)

    half_gains = gain_count // 2
    early = sum_dense(
        [
            by_device(grad_output_weight, 0),
            by_device(grad_router, 1),
            by_device(grad_gain_second, 0),
        ]
    )
    late = sum_dense([by_device(grad_inward, 0), by_device(grad_gain_first, 0)])
    grad_gains = jnp.stack(
        [
            late[inward_count : inward_count + half_gains],
            early[output_count + router_count : output_count + router_count + half_gains],
        ]
    )
    expert_sums = jnp.concatenate(chunk_sums, axis=0).astype(jnp.float32)
    return (
        output,
        grad_inputs.reshape(tokens.shape),
        grad_gains,
        late[:inward_count].reshape(query_key_value.shape),
        early[:output_count].reshape(attn_output.shape),
        early[output_count : output_count + router_count].reshape(router_weight.shape),
        expert_sums[:, :2],
        expert_sums[:, 2],
    )


def solution(mesh):
    placed = (
        P(("fsdp", "tp"), "ctx", None),
        P("fsdp", "ctx", None),
        P(("fsdp", "tp"), "ctx", None),
        P(None, ("fsdp", "ctx", "tp")),
        P(("fsdp", "ctx", "tp"), None),
        P(("fsdp", "ctx", "tp"), None),
        P(None, ("fsdp", "ctx", "tp")),
        P(None, None, ("fsdp", "ctx"), "tp"),
        P(None, ("fsdp", "ctx"), "tp"),
    )
    return jax.shard_map(
        per_device,
        mesh=mesh,
        in_specs=placed,
        out_specs=(
            P(("fsdp", "tp"), "ctx", None),
            P(("fsdp", "tp"), "ctx", None),
            P(None, ("fsdp", "ctx", "tp")),
            P(("fsdp", "ctx", "tp"), None),
            P(("fsdp", "ctx", "tp"), None),
            P(None, ("fsdp", "ctx", "tp")),
            P(None, None, ("fsdp", "ctx"), "tp"),
            P(None, ("fsdp", "ctx"), "tp"),
        ),
        check_vma=False,
    )
```

```python
import functools

import jax
import jax.numpy as jnp
from jax import lax
from jax.experimental import pallas as pl
from jax.experimental.layout import Layout, with_layout_constraint
from jax.experimental.pallas import tpu as pltpu
from jax.sharding import PartitionSpec as P

HEADS = 16
KV_HEADS = 8
HEAD = 64
EXPERTS = 32
TOP = 8


EPS = 1e-06
NEG = -1e30
HIGH = lax.Precision.HIGHEST
ALL_AXES = ("fsdp", "ctx", "tp")
CHUNKS = 4
TILE = 512
LANES = 128


def times_transposed(left_side, right_side):
    return lax.dot_general(
        left_side, right_side, (((1,), (1,)), ((), ())), preferred_element_type=jnp.float32
    )


def transposed_times(left_side, right_side):
    return lax.dot_general(
        left_side, right_side, (((0,), (0,)), ((), ())), preferred_element_type=jnp.float32
    )


def angle_tables(positions, head_size):
    half_size = head_size // 2
    inverse = 10000.0 ** (-jnp.arange(half_size, dtype=jnp.float32) * 2.0 / head_size)
    angles = positions.astype(jnp.float32)[:, None] * inverse[None, :]
    return (jnp.cos(angles), jnp.sin(angles))


def rotary(values, cosine_table, sine_table):
    half_size = values.shape[-1] // 2
    former = values[..., :half_size]
    latter = values[..., half_size:]
    return jnp.concatenate(
        [former * cosine_table - latter * sine_table, latter * cosine_table + former * sine_table],
        axis=-1,
    )


def rotary_back(gradient, cosine_table, sine_table):
    half_size = gradient.shape[-1] // 2
    former = gradient[..., :half_size]
    latter = gradient[..., half_size:]
    return jnp.concatenate(
        [former * cosine_table + latter * sine_table, latter * cosine_table - former * sine_table],
        axis=-1,
    )


def rms_back(grad_normed, normed, inverse, gain_row):
    scaled_grad = grad_normed * gain_row
    return inverse * (scaled_grad - normed * jnp.mean(scaled_grad * normed, axis=1, keepdims=True))


def by_rows(array):
    return with_layout_constraint(array, Layout(tuple(range(array.ndim))))


def dot_nn(left_side, right_side):
    return lax.dot_general(
        left_side, right_side, (((1,), (0,)), ((), ())), preferred_element_type=jnp.float32
    )


def pack_rows(pieces, width):
    flat = jnp.concatenate([piece.reshape(-1) for piece in pieces])
    rows = -(-flat.shape[0] // (16 * width)) * 16
    return jnp.pad(flat, (0, rows * width - flat.shape[0])).reshape(rows, width)


def expert_kernel(first, steps, base_expert, extra, places_ref, *refs):
    count = len(steps)
    weight_refs, refs = refs[:count], refs[count:]
    rows_ref, rows_turned_ref, grad_ref, grad_turned_ref, gate_ref = refs[:5]
    refs = refs[5:]
    if not first:
        moe_in_ref, back_in_ref = refs[:2]
        refs = refs[2:]
    refs = refs[extra:]
    moe_ref, back_ref, choice_ref = refs[:3]
    out_refs, refs = refs[3 : 3 + count], refs[3 + count + extra :]
    moe, back, weight_in, weight_out, hidden_rows, grad_hidden, stage, semaphores = refs
    pair = pl.program_id(0)
    token_count = rows_ref.shape[0]
    units = weight_refs[0].shape[-1]
    depth = weight_refs[0].shape[-2]
    width = 2 * units

    last = pl.num_programs(0) - 1
    tiles = token_count // TILE

    def moves(tile, inward):
        rows = pl.ds(pl.multiple_of(tile * TILE, TILE), TILE)
        if inward:
            return (
                pltpu.make_async_copy(moe_in_ref.at[rows], moe.at[rows], semaphores.at[0, tile]),
                pltpu.make_async_copy(back_in_ref.at[rows], back.at[rows], semaphores.at[1, tile]),
            )
        return (
            pltpu.make_async_copy(moe.at[rows], moe_ref.at[rows], semaphores.at[2, tile]),
            pltpu.make_async_copy(back.at[rows], back_ref.at[rows], semaphores.at[3, tile]),
        )

    if not first:

        @pl.when(pair == 0)
        def _():
            for tile in range(tiles):
                for move in moves(tile, True):
                    move.start()

    @pl.when(pair == 0)
    def _():
        choice_ref[...] = jnp.zeros_like(choice_ref)
        if first:
            moe[...] = jnp.zeros_like(moe)
            back[...] = jnp.zeros_like(back)

    def place(number, block):
        return pl.ds(
            pl.multiple_of(places_ref[number] + block * steps[number], depth), depth
        )

    for number, ref in enumerate(weight_refs):
        for block in range(ref.shape[0]):
            where = place(number, block)
            for which in range(2):
                columns = slice(which * units, (which + 1) * units)
                weight_in[where, columns] = ref[block, which, 0]
                weight_in[where, width + which * units : width + (which + 1) * units] = ref[
                    block, which, 1
                ]
                weight_out[where, columns] = ref[block, which, 2]

    expert = base_expert + 2 * pair

    def tile_step(tile, carry):
        rows = pl.ds(pl.multiple_of(tile * TILE, TILE), TILE)
        both = dot_nn(rows_ref[rows, :], weight_in[...])
        probe = dot_nn(grad_ref[rows, :], weight_out[...])
        gates = gate_ref[rows, :]
        lane = lax.broadcasted_iota(jnp.int32, gates.shape, 1)
        pre_gate = both[:, :width]
        pre_up = both[:, width:]
        gate = jnp.concatenate(
            [
                jnp.broadcast_to(
                    jnp.sum(
                        jnp.where(lane == expert + which, gates, 0.0), axis=1, keepdims=True
                    ),
                    (TILE, units),
                )
                for which in range(2)
            ],
            axis=1,
        )
        sigmoid_gate = 1.0 / (1.0 + jnp.exp(-pre_gate))
        swish_gate = pre_gate * sigmoid_gate
        hidden = (swish_gate * pre_up).astype(jnp.bfloat16).astype(jnp.float32)
        gated = (hidden * gate).astype(jnp.bfloat16)
        product = probe * hidden
        choice = choice_ref[rows, :]
        for which in range(2):
            total = jnp.sum(
                product[:, which * units : (which + 1) * units], axis=1, keepdims=True
            )
            choice = jnp.where(lane == expert + which, total, choice)
        choice_ref[rows, :] = choice
        scaled = probe * gate
        grad_gate = (
            scaled * pre_up * sigmoid_gate * (1.0 + pre_gate * (1.0 - sigmoid_gate))
        ).astype(jnp.bfloat16)
        grad_up = (scaled * swish_gate).astype(jnp.bfloat16)
        hidden_rows[rows, :] = gated
        grad_hidden[rows, :width] = grad_gate
        grad_hidden[rows, width:] = grad_up
        if not first:

            @pl.when(pair == 0)
            def _():
                for move in moves(tile, True):
                    move.wait()

        moe[rows, :] += times_transposed(gated, weight_out[...])
        back[rows, :] += times_transposed(
            jnp.concatenate([grad_gate, grad_up], axis=1), weight_in[...]
        )

        @pl.when(pair == last)
        def _():
            for move in moves(tile, False):
                move.start()

        return carry

    lax.fori_loop(0, tiles, tile_step, 0)

    slab = 256

    def weight_step(tile, carry):
        rows = pl.ds(pl.multiple_of(tile * slab, slab), slab)
        stage[rows, : 2 * width] = dot_nn(rows_turned_ref[rows, :], grad_hidden[...]).astype(
            jnp.bfloat16
        )
        stage[rows, 2 * width :] = dot_nn(grad_turned_ref[rows, :], hidden_rows[...]).astype(
            jnp.bfloat16
        )
        return carry

    lax.fori_loop(0, rows_turned_ref.shape[0] // slab, weight_step, 0)

    for number, ref in enumerate(out_refs):
        for block in range(ref.shape[0]):
            where = place(number, block)
            for which in range(2):
                for kind in range(3):
                    start = kind * width + which * units
                    ref[block, which, kind] = stage[where, start : start + units]

    @pl.when(pair == last)
    def _():
        for tile in range(tiles):
            for move in moves(tile, False):
                move.wait()


def expert_pass(
    places, steps, weights, rows, rows_turned, grads, grads_turned, gates, totals, base_expert, earlier=()
):
    first = totals is None
    token_count, model_width = rows.shape
    experts, _, depth, units = weights[0].shape[1:]

    def whole(array):
        return pl.BlockSpec(
            array.shape, lambda *_: (0,) * array.ndim, pipeline_mode=pl.Buffered(1)
        )

    weight_specs = [
        pl.BlockSpec((piece.shape[0], 2, 3, depth, units), lambda pair, _: (0, pair, 0, 0, 0))
        for piece in weights
    ]
    operands = [*weights, rows, rows_turned, grads, grads_turned, gates]
    specs = [*weight_specs, *(whole(array) for array in operands[len(weights) :])]
    aliases = {}
    if not first:
        aliases = {1 + len(operands): 0, 2 + len(operands): 1}
        operands += list(totals)
        specs += [pl.BlockSpec(memory_space=pl.ANY)] * 2
    for number, array in enumerate(earlier):
        aliases[1 + len(operands)] = 3 + len(weights) + number
        operands.append(array)
        specs.append(pl.BlockSpec(memory_space=pl.ANY))
    total_shape = jax.ShapeDtypeStruct((token_count, model_width), jnp.float32)
    products = 2 * token_count * model_width * units * experts
    return pl.pallas_call(
        functools.partial(expert_kernel, first, steps, base_expert, len(earlier)),
        grid_spec=pltpu.PrefetchScalarGridSpec(
            num_scalar_prefetch=1,
            grid=(experts // 2,),
            in_specs=specs,
            out_specs=[
                pl.BlockSpec(memory_space=pl.ANY),
                pl.BlockSpec(memory_space=pl.ANY),
                pl.BlockSpec((token_count, LANES), lambda *_: (0, 0)),
                *weight_specs,
                *([pl.BlockSpec(memory_space=pl.ANY)] * len(earlier)),
            ],
            scratch_shapes=[
                pltpu.VMEM((token_count, model_width), jnp.float32),
                pltpu.VMEM((token_count, model_width), jnp.float32),
                pltpu.VMEM((model_width, 4 * units), jnp.bfloat16),
                pltpu.VMEM((model_width, 2 * units), jnp.bfloat16),
                pltpu.VMEM((token_count, 2 * units), jnp.bfloat16),
                pltpu.VMEM((token_count, 4 * units), jnp.bfloat16),
                pltpu.VMEM((model_width, 6 * units), jnp.bfloat16),
                pltpu.SemaphoreType.DMA((4, token_count // TILE)),
            ],
        ),
        out_shape=[
            total_shape,
            total_shape,
            jax.ShapeDtypeStruct((token_count, LANES), jnp.float32),
            *(jax.ShapeDtypeStruct(piece.shape, jnp.bfloat16) for piece in weights),
            *(jax.ShapeDtypeStruct(array.shape, array.dtype) for array in earlier),
        ],
        input_output_aliases=aliases,
        compiler_params=pltpu.CompilerParams(
            dimension_semantics=("arbitrary",), vmem_limit_bytes=60 * 2**20
        ),
        cost_estimate=pl.CostEstimate(
            flops=9 * products,
            bytes_accessed=40 * 2**20,
            transcendentals=token_count * units * experts,
        ),
    )(places, *operands)


def swap_pairs(count, bit):
    return [(index, index ^ bit) for index in range(count)]


def gather_group(rows):
    count = lax.axis_size("tp")
    across = lax.ppermute(rows, "tp", swap_pairs(count, 2))
    beside = lax.ppermute(rows, "tp", swap_pairs(count, 1))
    corner = lax.ppermute(across, "tp", swap_pairs(count, 1))
    return jnp.concatenate([rows, beside, across, corner], axis=0)


def scatter_group(terms):
    count = lax.axis_size("tp")
    parts = terms.reshape(count, -1, terms.shape[-1])
    first, second = (
        lax.ppermute(parts[which].astype(jnp.bfloat16), "tp", swap_pairs(count, 1)).astype(
            jnp.float32
        )
        for which in (3, 1)
    )
    passed = lax.ppermute((parts[2] + first).astype(jnp.bfloat16), "tp", swap_pairs(count, 2))
    return parts[0] + second + passed.astype(jnp.float32)


def shifted(count, step):
    return [(index, (index + step) % count) for index in range(count)]


def gather_axis(piece, name):
    count = lax.axis_size(name)
    mine = lax.axis_index(name)
    found = [piece] + [
        lax.ppermute(piece, name, shifted(count, -step)) for step in range(1, count)
    ]
    return lax.dynamic_slice_in_dim(
        jnp.stack(found + found[:-1]), (count - mine) % count, count, axis=0
    )


def gather_bit(piece, bit):
    other = lax.ppermute(piece, "tp", swap_pairs(lax.axis_size("tp"), bit))
    upper = (lax.axis_index("tp") & bit) > 0
    return jnp.where(upper, jnp.stack([other, piece]), jnp.stack([piece, other]))


def gather_dense(piece):
    fsdp_count, context_count = lax.axis_size("fsdp"), lax.axis_size("ctx")
    whole = gather_bit(gather_bit(gather_axis(gather_axis(piece, "fsdp"), "ctx"), 2), 1)
    whole = whole.reshape((2, 2, context_count, fsdp_count) + piece.shape)
    return whole.transpose(3, 2, 1, 0, 4, 5).reshape((-1,) + piece.shape)


def scatter_axis(parts, name):
    count = lax.axis_size(name)
    mine = lax.axis_index(name)
    low = parts.astype(jnp.bfloat16)
    total = lax.dynamic_index_in_dim(parts, mine, 0, keepdims=False).astype(jnp.float32)
    for step in range(1, count):
        sent = lax.dynamic_index_in_dim(low, (mine + step) % count, 0, keepdims=False)
        total = total + lax.ppermute(sent, name, shifted(count, step)).astype(jnp.float32)
    return total


def scatter_bit(parts, bit, axis):
    mine = (lax.axis_index("tp") & bit) // bit
    sent = lax.dynamic_index_in_dim(parts, 1 - mine, axis, keepdims=False).astype(jnp.bfloat16)
    kept = lax.dynamic_index_in_dim(parts, mine, axis, keepdims=False).astype(jnp.float32)
    return kept + lax.ppermute(sent, "tp", swap_pairs(lax.axis_size("tp"), bit)).astype(
        jnp.float32
    )


def scatter_dense(parts):
    fsdp_count, context_count = lax.axis_size("fsdp"), lax.axis_size("ctx")
    parts = parts.reshape((fsdp_count, context_count, 2, 2) + parts.shape[1:])
    parts = scatter_bit(scatter_bit(parts, 1, 3), 2, 2)
    return scatter_axis(scatter_axis(jnp.moveaxis(parts, 1, 0), "ctx"), "fsdp")


def hold(*refs):
    pass


def together(*values):
    spec = pl.BlockSpec(memory_space=pl.ANY)
    return pl.pallas_call(
        hold,
        in_specs=[spec] * len(values),
        out_specs=[spec] * len(values),
        out_shape=[jax.ShapeDtypeStruct(value.shape, value.dtype) for value in values],
        input_output_aliases={number: number for number in range(len(values))},
    )(*values)


def after(value, *earlier):
    spec = pl.BlockSpec(memory_space=pl.ANY)
    return pl.pallas_call(
        hold,
        in_specs=[spec] * (1 + len(earlier)),
        out_specs=spec,
        out_shape=jax.ShapeDtypeStruct(value.shape, value.dtype),
        input_output_aliases={0: 0},
    )(value, *earlier)


def per_device(
    tokens,
    routes,
    cotangent,
    norm_gains,
    query_key_value,
    attn_output,
    router_weight,
    expert_in,
    expert_out,
):
    local_seqs, local_positions, model_width = tokens.shape
    context_count = lax.axis_size("ctx")
    length = local_positions * context_count
    row_count = local_seqs * local_positions
    local_groups = KV_HEADS // context_count
    head_size = HEAD
    score_scale = HEAD ** (-0.5)
    capacity = local_positions * 3 // 8
    group_grads = by_rows(gather_group(cotangent.reshape(row_count, model_width)))
    grads_turned = by_rows(group_grads.T)
    device_count = context_count * lax.axis_size("fsdp") * lax.axis_size("tp")
    gain_count, router_count = norm_gains.size, router_weight.size
    packed = lax.all_gather(pack_rows([query_key_value, norm_gains], model_width), ALL_AXES, axis=0)
    packed = after(packed, grads_turned)
    packed_later = gather_dense(pack_rows([attn_output, router_weight], model_width))
    inward_rows, output_rows = query_key_value.shape[0], attn_output.shape[0]
    inward_full = packed[:, :inward_rows].reshape(-1, model_width)
    gain_full = (
        packed[:, inward_rows:]
        .reshape(device_count, -1)[:, :gain_count]
        .reshape(device_count, 2, -1)
        .transpose(1, 0, 2)
        .reshape(2, model_width)
    )
    output_full = packed_later[:, :output_rows].reshape(-1, model_width)
    router_full = (
        packed_later[:, output_rows:]
        .reshape(device_count, -1)[:, :router_count]
        .reshape(device_count, EXPERTS, -1)
        .transpose(1, 0, 2)
        .reshape(EXPERTS, model_width)
    )
    paired = context_count == 2
    expert_shards = jnp.concatenate([expert_in, expert_out[:, None]], axis=1)
    shard_depth = expert_in.shape[2]
    chunk_experts = EXPERTS // CHUNKS
    my_context = lax.axis_index("ctx").astype(jnp.int32)
    if paired:
        places = jnp.stack([my_context, 1 - my_context]) * shard_depth
        steps = (2 * shard_depth, 2 * shard_depth)
    else:
        places = jnp.zeros((1,), jnp.int32)
        steps = (shard_depth,)
    expert_pieces = []
    for chunk in range(CHUNKS):
        shard = expert_shards[chunk * chunk_experts : (chunk + 1) * chunk_experts]
        if paired:
            expert_pieces.append([lax.all_gather(shard, "fsdp", axis=0)])
            if chunk == CHUNKS - 1:
                other = lax.ppermute(shard, "ctx", swap_pairs(2, 1))
                expert_pieces[chunk].append(lax.all_gather(other, "fsdp", axis=0))
        else:
            expert_pieces.append([lax.all_gather(shard, ("fsdp", "ctx"), axis=0)])
    gain_rows = gain_full.astype(jnp.float32)
    inputs = tokens.astype(jnp.float32).reshape(row_count, model_width)
    inverse_first = lax.rsqrt(jnp.mean(inputs * inputs, axis=1, keepdims=True) + EPS)
    normed_first = inputs * inverse_first
    first_low = (normed_first * gain_rows[0]).astype(jnp.bfloat16)
    projected = times_transposed(first_low, inward_full).reshape(
        local_seqs, local_positions, KV_HEADS, 4, head_size
    )
    positions = lax.axis_index("ctx") * local_positions + jnp.arange(
        local_positions, dtype=jnp.int32
    )
    cosine_table, sine_table = angle_tables(positions, head_size)
    cosine_rows = cosine_table[None, :, None, None, :]
    sine_rows = sine_table[None, :, None, None, :]
    turned = jnp.concatenate(
        [rotary(projected[:, :, :, :3], cosine_rows, sine_rows), projected[:, :, :, 3:]], axis=3
    )
    sent_heads = turned.astype(jnp.bfloat16).reshape(
        local_seqs, local_positions, KV_HEADS, 4 * head_size
    )
    head_rows = lax.all_to_all(sent_heads, "ctx", split_axis=2, concat_axis=1, tiled=True)
    queries = head_rows[..., : 2 * head_size].reshape(
        local_seqs, length, local_groups, 2, head_size
    )
    key_rows = head_rows[..., 2 * head_size : 3 * head_size]
    value_rows = head_rows[..., 3 * head_size :]
    block_rows = min(512, length)
    key_index = jnp.arange(length)
    attended = []
    log_totals = []
    for offset in range(0, length, block_rows):
        limit_row = offset + block_rows
        scores = (
            jnp.einsum(
                "sqgjd,skgd->sgjqk",
                queries[:, offset:limit_row],
                key_rows[:, :limit_row],
                preferred_element_type=jnp.float32,
            )
            * score_scale
        )
        visible = (offset + jnp.arange(block_rows))[:, None] >= key_index[None, :limit_row]
        scores = jnp.where(visible, scores, NEG)
        top_score = jnp.max(scores, axis=-1, keepdims=True)
        exponent = jnp.exp(scores - top_score)
        denominator = jnp.sum(exponent, axis=-1, keepdims=True)
        weights = exponent / denominator
        attended.append(
            jnp.einsum(
                "sgjqk,skgd->sqgjd",
                weights.astype(jnp.bfloat16),
                value_rows[:, :limit_row],
                preferred_element_type=jnp.float32,
            )
        )
        log_totals.append(top_score + jnp.log(denominator))
    head_output = (
        jnp.concatenate(attended, axis=1)
        .astype(jnp.bfloat16)
        .reshape(local_seqs, length, local_groups, 2 * head_size)
    )
    merged = lax.all_to_all(head_output, "ctx", split_axis=1, concat_axis=2, tiled=True).reshape(
        row_count, HEADS * head_size
    )
    hidden = inputs + times_transposed(merged, output_full)
    inverse_second = lax.rsqrt(jnp.mean(hidden * hidden, axis=1, keepdims=True) + EPS)
    normed_second = hidden * inverse_second
    second_low = (normed_second * gain_rows[1]).astype(jnp.bfloat16)
    group_rows = by_rows(gather_group(by_rows(second_low)))
    group_count = group_rows.shape[0]
    chances = jax.nn.softmax(times_transposed(group_rows, router_full), axis=-1)
    group_order = jnp.bitwise_xor(
        jnp.arange(lax.axis_size("tp"), dtype=jnp.int32), lax.axis_index("tp").astype(jnp.int32)
    )
    route_rows = jnp.take(
        routes.reshape(lax.axis_size("tp"), row_count, TOP), group_order, axis=0
    ).reshape(group_count, TOP)
    chosen_any = jnp.sum(
        (route_rows[:, :, None] == jnp.arange(EXPERTS, dtype=jnp.int32)[None, None, :]).astype(
            jnp.float32
        ),
        axis=1,
    )
    gates = jnp.pad(chances * chosen_any, ((0, 0), (0, LANES - EXPERTS)))
    group_turned = by_rows(group_rows.T)
    totals = None
    choice_total = None
    chunk_sums = []
    own_sums = []
    far_sums = []
    arrivals = []
    marks = []

    def fetch(chunk):
        near = expert_pieces[chunk][0]
        if chunk > 1:
            near = after(near, marks[chunk - 2])
            expert_pieces[chunk][0] = near
        expert_pieces[chunk].append(lax.ppermute(near, "ctx", swap_pairs(2, 1)))

    if paired:
        fetch(0)
    for chunk in range(CHUNKS):
        if paired:
            if chunk + 2 < CHUNKS:
                fetch(chunk + 1)
        moe_total, back_total, choice, *grad_pieces = expert_pass(
            places,
            steps,
            expert_pieces[chunk],
            group_rows,
            group_turned,
            group_grads,
            grads_turned,
            gates,
            totals,
            chunk * chunk_experts,
        )
        totals = (moe_total, back_total)
        marks.append(choice)
        choice_total = choice if choice_total is None else choice_total + choice
        if paired:
            own_sums.append(grad_pieces[0])
            far_sums.append(grad_pieces[1])
        else:
            chunk_sums.append(
                lax.psum_scatter(grad_pieces[0], ("fsdp", "ctx"), scatter_dimension=0)
            )
    if paired:
        for chunk in range(CHUNKS - 1):
            held = after(far_sums[chunk], marks[min(chunk + 1, CHUNKS - 1)])
            arrivals.append(lax.ppermute(held, "ctx", swap_pairs(2, 1)))
        last_sums = [
            lax.psum_scatter(part, "fsdp", scatter_dimension=0)
            for part in (far_sums[-1], own_sums[-1])
        ]
    grad_chances = choice_total[:, :EXPERTS] * chosen_any
    grad_logits = chances * (grad_chances - jnp.sum(grad_chances * chances, axis=-1, keepdims=True))
    router_rows = router_full.astype(jnp.float32)
    grad_router = jnp.dot(grad_logits.T, group_rows.astype(jnp.float32), precision=HIGH)
    back_group = by_rows(totals[1] + jnp.dot(grad_logits, router_rows, precision=HIGH))
    grad_second = by_rows(scatter_group(back_group))
    moe_rows = by_rows(scatter_group(totals[0]))
    output = (hidden + moe_rows).astype(jnp.bfloat16).reshape(tokens.shape)
    grad_gain_second = jnp.sum(grad_second * normed_second, axis=0)
    grad_hidden = cotangent.astype(jnp.float32).reshape(row_count, model_width) + rms_back(
        grad_second, normed_second, inverse_second, gain_rows[1]
    )
    grad_attn = by_rows(grad_hidden.astype(jnp.bfloat16))
    if paired:
        grad_attn, arrivals[0] = together(grad_attn, arrivals[0])
    grad_output_weight = transposed_times(grad_attn, merged)
    grad_merged = (
        jnp.dot(grad_attn, output_full, preferred_element_type=jnp.float32)
        .astype(jnp.bfloat16)
        .reshape(local_seqs, local_positions, KV_HEADS, 2 * head_size)
    )
    grad_heads = lax.all_to_all(by_rows(grad_merged), "ctx", split_axis=2, concat_axis=1, tiled=True)
    grad_keys = jnp.zeros((local_seqs, length, local_groups, head_size), jnp.float32)
    grad_values = jnp.zeros((local_seqs, length, local_groups, head_size), jnp.float32)
    grad_query_blocks = []
    for offset, log_total in zip(range(0, length, block_rows), log_totals):
        limit_row = offset + block_rows
        query_block = queries[:, offset:limit_row]
        key_part = key_rows[:, :limit_row]
        value_part = value_rows[:, :limit_row]
        scores = (
            jnp.einsum(
                "sqgjd,skgd->sgjqk", query_block, key_part, preferred_element_type=jnp.float32
            )
            * score_scale
        )
        visible = (offset + jnp.arange(block_rows))[:, None] >= key_index[None, :limit_row]
        scores = jnp.where(visible, scores, NEG)
        weights = jnp.exp(scores - log_total)
        grad_block = grad_heads[:, offset:limit_row].reshape(
            local_seqs, block_rows, local_groups, 2, head_size
        )
        grad_values = grad_values.at[:, :limit_row].add(
            jnp.einsum(
                "sgjqk,sqgjd->skgd",
                weights.astype(jnp.bfloat16),
                grad_block,
                preferred_element_type=jnp.float32,
            )
        )
        grad_weights = jnp.einsum(
            "sqgjd,skgd->sgjqk", grad_block, value_part, preferred_element_type=jnp.float32
        )
        grad_scores = (
            weights * (grad_weights - jnp.sum(weights * grad_weights, axis=-1, keepdims=True))
        ).astype(jnp.bfloat16)
        grad_query_blocks.append(
            jnp.einsum(
                "sgjqk,skgd->sqgjd", grad_scores, key_part, preferred_element_type=jnp.float32
            )
            * score_scale
        )
        grad_keys = grad_keys.at[:, :limit_row].add(
            jnp.einsum(
                "sgjqk,sqgjd->skgd", grad_scores, query_block, preferred_element_type=jnp.float32
            )
            * score_scale
        )
    grad_queries = jnp.concatenate(grad_query_blocks, axis=1).reshape(
        local_seqs, length, local_groups, 2 * head_size
    )
    grad_head_rows = jnp.concatenate([grad_queries, grad_keys, grad_values], axis=-1).astype(
        jnp.bfloat16
    )
    if paired:
        grad_head_rows, arrivals[1] = together(grad_head_rows, arrivals[1])
        for own, arrived in zip(own_sums, arrivals):
            joined = (own.astype(jnp.float32) + arrived.astype(jnp.float32)).astype(jnp.bfloat16)
            chunk_sums.append(lax.psum_scatter(joined, "fsdp", scatter_dimension=0))
        far = lax.ppermute(last_sums[0], "ctx", swap_pairs(2, 1))
        chunk_sums.append(last_sums[1].astype(jnp.float32) + far.astype(jnp.float32))
    grad_turned = (
        lax.all_to_all(grad_head_rows, "ctx", split_axis=1, concat_axis=2, tiled=True)
        .astype(jnp.float32)
        .reshape(local_seqs, local_positions, KV_HEADS, 4, head_size)
    )
    grad_projected = (
        jnp.concatenate(
            [
                rotary_back(grad_turned[:, :, :, :3], cosine_rows, sine_rows),
                grad_turned[:, :, :, 3:],
            ],
            axis=3,
        )
        .astype(jnp.bfloat16)
        .reshape(row_count, -1)
    )
    grad_inward = transposed_times(grad_projected, first_low)
    grad_first = jnp.dot(grad_projected, inward_full, preferred_element_type=jnp.float32)
    grad_gain_first = jnp.sum(grad_first * normed_first, axis=0)
    grad_inputs = grad_hidden + rms_back(grad_first, normed_first, inverse_first, gain_rows[0])
    grad_gains = jnp.stack([grad_gain_first, grad_gain_second])

    def by_device(array, axis):
        parts = array.reshape(
            array.shape[:axis] + (device_count, -1) + array.shape[axis + 1 :]
        )
        return jnp.moveaxis(parts, axis, 0).reshape(device_count, -1)

    inward_sum = scatter_dense(
        grad_inward.astype(jnp.bfloat16).reshape((device_count,) + query_key_value.shape)
    )
    output_sum = scatter_dense(
        grad_output_weight.astype(jnp.bfloat16).reshape((device_count,) + attn_output.shape)
    )
    small = jnp.concatenate([by_device(grad_router, 1), by_device(grad_gains, 1)], axis=1)
    small_count = small.shape[1]
    small_rows = -(-small_count // (16 * LANES)) * 16
    small = jnp.pad(small, ((0, 0), (0, small_rows * LANES - small_count)))
    small_sum = scatter_dense(small.reshape(device_count, small_rows, LANES)).reshape(-1)
    expert_sums = jnp.concatenate([part.astype(jnp.float32) for part in chunk_sums], axis=0)
    return (
        output,
        grad_inputs.reshape(tokens.shape),
        small_sum[router_count:small_count].reshape(norm_gains.shape),
        inward_sum,
        output_sum,
        small_sum[:router_count].reshape(router_weight.shape),
        expert_sums[:, :2],
        expert_sums[:, 2],
    )


def solution(mesh):
    placed = (
        P(("fsdp", "tp"), "ctx", None),
        P("fsdp", "ctx", None),
        P(("fsdp", "tp"), "ctx", None),
        P(None, ("fsdp", "ctx", "tp")),
        P(("fsdp", "ctx", "tp"), None),
        P(("fsdp", "ctx", "tp"), None),
        P(None, ("fsdp", "ctx", "tp")),
        P(None, None, ("fsdp", "ctx"), "tp"),
        P(None, ("fsdp", "ctx"), "tp"),
    )
    return jax.shard_map(
        per_device,
        mesh=mesh,
        in_specs=placed,
        out_specs=(
            P(("fsdp", "tp"), "ctx", None),
            P(("fsdp", "tp"), "ctx", None),
            P(None, ("fsdp", "ctx", "tp")),
            P(("fsdp", "ctx", "tp"), None),
            P(("fsdp", "ctx", "tp"), None),
            P(None, ("fsdp", "ctx", "tp")),
            P(None, None, ("fsdp", "ctx"), "tp"),
            P(None, ("fsdp", "ctx"), "tp"),
        ),
        check_vma=False,
    )
```

```python
import functools

import jax
import jax.numpy as jnp
from jax import lax
from jax.experimental import pallas as pl
from jax.experimental.layout import Layout, with_layout_constraint
from jax.experimental.pallas import tpu as pltpu
from jax.sharding import PartitionSpec as P

HEADS = 16
KV_HEADS = 8
HEAD = 64
EXPERTS = 32
TOP = 8


EPS = 1e-06
NEG = -1e30
HIGH = lax.Precision.HIGHEST
ALL_AXES = ("fsdp", "ctx", "tp")
CHUNKS = 4
TILE = 512
LANES = 128


def times_transposed(left_side, right_side):
    return lax.dot_general(
        left_side, right_side, (((1,), (1,)), ((), ())), preferred_element_type=jnp.float32
    )


def transposed_times(left_side, right_side):
    return lax.dot_general(
        left_side, right_side, (((0,), (0,)), ((), ())), preferred_element_type=jnp.float32
    )


def angle_tables(positions, head_size):
    half_size = head_size // 2
    inverse = 10000.0 ** (-jnp.arange(half_size, dtype=jnp.float32) * 2.0 / head_size)
    angles = positions.astype(jnp.float32)[:, None] * inverse[None, :]
    return (jnp.cos(angles), jnp.sin(angles))


def rotary(values, cosine_table, sine_table):
    half_size = values.shape[-1] // 2
    former = values[..., :half_size]
    latter = values[..., half_size:]
    return jnp.concatenate(
        [former * cosine_table - latter * sine_table, latter * cosine_table + former * sine_table],
        axis=-1,
    )


def rotary_back(gradient, cosine_table, sine_table):
    half_size = gradient.shape[-1] // 2
    former = gradient[..., :half_size]
    latter = gradient[..., half_size:]
    return jnp.concatenate(
        [former * cosine_table + latter * sine_table, latter * cosine_table - former * sine_table],
        axis=-1,
    )


def rms_back(grad_normed, normed, inverse, gain_row):
    scaled_grad = grad_normed * gain_row
    return inverse * (scaled_grad - normed * jnp.mean(scaled_grad * normed, axis=1, keepdims=True))


def by_rows(array):
    return with_layout_constraint(array, Layout(tuple(range(array.ndim))))


def dot_nn(left_side, right_side):
    return lax.dot_general(
        left_side, right_side, (((1,), (0,)), ((), ())), preferred_element_type=jnp.float32
    )


def pack_rows(pieces, width):
    flat = jnp.concatenate([piece.reshape(-1) for piece in pieces])
    rows = -(-flat.shape[0] // (16 * width)) * 16
    return jnp.pad(flat, (0, rows * width - flat.shape[0])).reshape(rows, width)


def expert_kernel(first, steps, base_expert, extra, places_ref, *refs):
    count = len(steps)
    weight_refs, refs = refs[:count], refs[count:]
    rows_ref, rows_turned_ref, grad_ref, grad_turned_ref, gate_ref = refs[:5]
    refs = refs[5:]
    if not first:
        moe_in_ref, back_in_ref = refs[:2]
        refs = refs[2:]
    refs = refs[extra:]
    moe_ref, back_ref, choice_ref = refs[:3]
    out_refs, refs = refs[3 : 3 + count], refs[3 + count + extra :]
    moe, back, weight_in, weight_out, hidden_rows, grad_hidden, stage, semaphores = refs
    pair = pl.program_id(0)
    token_count = rows_ref.shape[0]
    units = weight_refs[0].shape[-1]
    depth = weight_refs[0].shape[-2]
    width = 2 * units

    last = pl.num_programs(0) - 1
    tiles = token_count // TILE

    def moves(tile, inward):
        rows = pl.ds(pl.multiple_of(tile * TILE, TILE), TILE)
        if inward:
            return (
                pltpu.make_async_copy(moe_in_ref.at[rows], moe.at[rows], semaphores.at[0, tile]),
                pltpu.make_async_copy(back_in_ref.at[rows], back.at[rows], semaphores.at[1, tile]),
            )
        return (
            pltpu.make_async_copy(moe.at[rows], moe_ref.at[rows], semaphores.at[2, tile]),
            pltpu.make_async_copy(back.at[rows], back_ref.at[rows], semaphores.at[3, tile]),
        )

    if not first:

        @pl.when(pair == 0)
        def _():
            for tile in range(tiles):
                for move in moves(tile, True):
                    move.start()

    @pl.when(pair == 0)
    def _():
        choice_ref[...] = jnp.zeros_like(choice_ref)
        if first:
            moe[...] = jnp.zeros_like(moe)
            back[...] = jnp.zeros_like(back)

    def place(number, block):
        return pl.ds(
            pl.multiple_of(places_ref[number] + block * steps[number], depth), depth
        )

    for number, ref in enumerate(weight_refs):
        for block in range(ref.shape[0]):
            where = place(number, block)
            for which in range(2):
                columns = slice(which * units, (which + 1) * units)
                weight_in[where, columns] = ref[block, which, 0]
                weight_in[where, width + which * units : width + (which + 1) * units] = ref[
                    block, which, 1
                ]
                weight_out[where, columns] = ref[block, which, 2]

    expert = base_expert + 2 * pair

    def tile_step(tile, carry):
        rows = pl.ds(pl.multiple_of(tile * TILE, TILE), TILE)
        both = dot_nn(rows_ref[rows, :], weight_in[...])
        probe = dot_nn(grad_ref[rows, :], weight_out[...])
        gates = gate_ref[rows, :]
        lane = lax.broadcasted_iota(jnp.int32, gates.shape, 1)
        pre_gate = both[:, :width]
        pre_up = both[:, width:]
        gate = jnp.concatenate(
            [
                jnp.broadcast_to(
                    jnp.sum(
                        jnp.where(lane == expert + which, gates, 0.0), axis=1, keepdims=True
                    ),
                    (TILE, units),
                )
                for which in range(2)
            ],
            axis=1,
        )
        sigmoid_gate = 1.0 / (1.0 + jnp.exp(-pre_gate))
        swish_gate = pre_gate * sigmoid_gate
        hidden = (swish_gate * pre_up).astype(jnp.bfloat16).astype(jnp.float32)
        gated = (hidden * gate).astype(jnp.bfloat16)
        product = probe * hidden
        choice = choice_ref[rows, :]
        for which in range(2):
            total = jnp.sum(
                product[:, which * units : (which + 1) * units], axis=1, keepdims=True
            )
            choice = jnp.where(lane == expert + which, total, choice)
        choice_ref[rows, :] = choice
        scaled = probe * gate
        grad_gate = (
            scaled * pre_up * sigmoid_gate * (1.0 + pre_gate * (1.0 - sigmoid_gate))
        ).astype(jnp.bfloat16)
        grad_up = (scaled * swish_gate).astype(jnp.bfloat16)
        hidden_rows[rows, :] = gated
        grad_hidden[rows, :width] = grad_gate
        grad_hidden[rows, width:] = grad_up
        if not first:

            @pl.when(pair == 0)
            def _():
                for move in moves(tile, True):
                    move.wait()

        moe[rows, :] += times_transposed(gated, weight_out[...])
        back[rows, :] += times_transposed(
            jnp.concatenate([grad_gate, grad_up], axis=1), weight_in[...]
        )

        @pl.when(pair == last)
        def _():
            for move in moves(tile, False):
                move.start()

        return carry

    lax.fori_loop(0, tiles, tile_step, 0, unroll=True)

    slab = 512

    def weight_step(tile, carry):
        rows = pl.ds(pl.multiple_of(tile * slab, slab), slab)
        stage[rows, : 2 * width] = dot_nn(rows_turned_ref[rows, :], grad_hidden[...]).astype(
            jnp.bfloat16
        )
        stage[rows, 2 * width :] = dot_nn(grad_turned_ref[rows, :], hidden_rows[...]).astype(
            jnp.bfloat16
        )
        return carry

    lax.fori_loop(0, rows_turned_ref.shape[0] // slab, weight_step, 0)

    for number, ref in enumerate(out_refs):
        for block in range(ref.shape[0]):
            where = place(number, block)
            for which in range(2):
                for kind in range(3):
                    start = kind * width + which * units
                    ref[block, which, kind] = stage[where, start : start + units]

    @pl.when(pair == last)
    def _():
        for tile in range(tiles):
            for move in moves(tile, False):
                move.wait()


def expert_pass(
    places, steps, weights, rows, rows_turned, grads, grads_turned, gates, totals, base_expert, earlier=()
):
    first = totals is None
    token_count, model_width = rows.shape
    experts, _, depth, units = weights[0].shape[1:]

    def whole(array):
        return pl.BlockSpec(
            array.shape, lambda *_: (0,) * array.ndim, pipeline_mode=pl.Buffered(1)
        )

    weight_specs = [
        pl.BlockSpec((piece.shape[0], 2, 3, depth, units), lambda pair, _: (0, pair, 0, 0, 0))
        for piece in weights
    ]
    operands = [*weights, rows, rows_turned, grads, grads_turned, gates]
    specs = [*weight_specs, *(whole(array) for array in operands[len(weights) :])]
    aliases = {}
    if not first:
        aliases = {1 + len(operands): 0, 2 + len(operands): 1}
        operands += list(totals)
        specs += [pl.BlockSpec(memory_space=pl.ANY)] * 2
    for number, array in enumerate(earlier):
        aliases[1 + len(operands)] = 3 + len(weights) + number
        operands.append(array)
        specs.append(pl.BlockSpec(memory_space=pl.ANY))
    total_shape = jax.ShapeDtypeStruct((token_count, model_width), jnp.float32)
    products = 2 * token_count * model_width * units * experts
    return pl.pallas_call(
        functools.partial(expert_kernel, first, steps, base_expert, len(earlier)),
        grid_spec=pltpu.PrefetchScalarGridSpec(
            num_scalar_prefetch=1,
            grid=(experts // 2,),
            in_specs=specs,
            out_specs=[
                pl.BlockSpec(memory_space=pl.ANY),
                pl.BlockSpec(memory_space=pl.ANY),
                pl.BlockSpec((token_count, LANES), lambda *_: (0, 0)),
                *weight_specs,
                *([pl.BlockSpec(memory_space=pl.ANY)] * len(earlier)),
            ],
            scratch_shapes=[
                pltpu.VMEM((token_count, model_width), jnp.float32),
                pltpu.VMEM((token_count, model_width), jnp.float32),
                pltpu.VMEM((model_width, 4 * units), jnp.bfloat16),
                pltpu.VMEM((model_width, 2 * units), jnp.bfloat16),
                pltpu.VMEM((token_count, 2 * units), jnp.bfloat16),
                pltpu.VMEM((token_count, 4 * units), jnp.bfloat16),
                pltpu.VMEM((model_width, 6 * units), jnp.bfloat16),
                pltpu.SemaphoreType.DMA((4, token_count // TILE)),
            ],
        ),
        out_shape=[
            total_shape,
            total_shape,
            jax.ShapeDtypeStruct((token_count, LANES), jnp.float32),
            *(jax.ShapeDtypeStruct(piece.shape, jnp.bfloat16) for piece in weights),
            *(jax.ShapeDtypeStruct(array.shape, array.dtype) for array in earlier),
        ],
        input_output_aliases=aliases,
        compiler_params=pltpu.CompilerParams(
            dimension_semantics=("arbitrary",), vmem_limit_bytes=60 * 2**20
        ),
        cost_estimate=pl.CostEstimate(
            flops=9 * products,
            bytes_accessed=40 * 2**20,
            transcendentals=token_count * units * experts,
        ),
    )(places, *operands)


def visible_mask(first_row, first_key, row_count, key_count):
    rows = first_row + lax.broadcasted_iota(jnp.int32, (row_count, key_count), 0)
    keys = first_key + lax.broadcasted_iota(jnp.int32, (row_count, key_count), 1)
    return rows >= keys


def attend_kernel(block, heads_ref, out_ref, log_ref):
    length = heads_ref.shape[1]
    keys = heads_ref[0, :, 2 * HEAD : 3 * HEAD]
    values = heads_ref[0, :, 3 * HEAD :]
    for offset in range(0, length, block):
        limit = offset + block
        mask = visible_mask(offset, 0, block, limit)
        for which in range(2):
            lanes = slice(which * HEAD, (which + 1) * HEAD)
            query = heads_ref[0, offset:limit, lanes]
            scores = times_transposed(query, keys[:limit]) * HEAD ** (-0.5)
            scores = jnp.where(mask, scores, NEG)
            top_score = jnp.max(scores, axis=1, keepdims=True)
            exponent = jnp.exp(scores - top_score)
            denominator = jnp.sum(exponent, axis=1, keepdims=True)
            weights = (exponent * (1.0 / denominator)).astype(jnp.bfloat16)
            out_ref[0, offset:limit, lanes] = dot_nn(weights, values[:limit]).astype(jnp.bfloat16)
            log_ref[0, 0, offset:limit, which : which + 1] = top_score + jnp.log(denominator)


def attend_back_kernel(block, heads_ref, grad_ref, log_ref, out_ref, grad_keys, grad_values):
    length = heads_ref.shape[1]
    grad_keys[...] = jnp.zeros_like(grad_keys)
    grad_values[...] = jnp.zeros_like(grad_values)
    keys = heads_ref[0, :, 2 * HEAD : 3 * HEAD]
    values = heads_ref[0, :, 3 * HEAD :]
    for offset in range(0, length, block):
        limit = offset + block
        mask = visible_mask(offset, 0, block, limit)
        for which in range(2):
            lanes = slice(which * HEAD, (which + 1) * HEAD)
            query = heads_ref[0, offset:limit, lanes]
            grad = grad_ref[0, offset:limit, lanes]
            scores = times_transposed(query, keys[:limit]) * HEAD ** (-0.5)
            log_total = log_ref[0, 0, offset:limit, which : which + 1]
            weights = jnp.where(mask, jnp.exp(jnp.where(mask, scores, NEG) - log_total), 0.0)
            grad_weights = times_transposed(grad, values[:limit])
            middle = jnp.sum(weights * grad_weights, axis=1, keepdims=True)
            grad_scores = (weights * (grad_weights - middle)).astype(jnp.bfloat16)
            grad_values[:limit, :] += transposed_times(weights.astype(jnp.bfloat16), grad)
            grad_keys[:limit, :] += transposed_times(grad_scores, query)
            out_ref[0, offset:limit, lanes] = (
                dot_nn(grad_scores, keys[:limit]) * HEAD ** (-0.5)
            ).astype(jnp.bfloat16)
    out_ref[0, :, 2 * HEAD : 3 * HEAD] = (grad_keys[...] * HEAD ** (-0.5)).astype(jnp.bfloat16)
    out_ref[0, :, 3 * HEAD :] = grad_values[...].astype(jnp.bfloat16)


def attend(head_rows, grad_rows=None, log_totals=None):
    sequences, length, width = head_rows.shape
    groups = width // (4 * HEAD)
    block = min(256, length)

    def per_group(lane_count):
        return pl.BlockSpec((1, length, lane_count), lambda s, g: (s, 0, g))

    logs = pl.BlockSpec((1, 1, length, 2), lambda s, g: (s, g, 0, 0))
    work = sequences * groups * length * length * HEAD * 2
    params = pltpu.CompilerParams(
        dimension_semantics=("arbitrary", "arbitrary"), vmem_limit_bytes=48 * 2**20
    )
    if grad_rows is None:
        return pl.pallas_call(
            functools.partial(attend_kernel, block),
            grid=(sequences, groups),
            in_specs=[per_group(4 * HEAD)],
            out_specs=[per_group(2 * HEAD), logs],
            out_shape=[
                jax.ShapeDtypeStruct((sequences, length, groups * 2 * HEAD), jnp.bfloat16),
                jax.ShapeDtypeStruct((sequences, groups, length, 2), jnp.float32),
            ],
            compiler_params=params,
            cost_estimate=pl.CostEstimate(
                flops=16 * work, bytes_accessed=8 * 2**20, transcendentals=work // HEAD
            ),
        )(head_rows)
    return pl.pallas_call(
        functools.partial(attend_back_kernel, block),
        grid=(sequences, groups),
        in_specs=[per_group(4 * HEAD), per_group(2 * HEAD), logs],
        out_specs=per_group(4 * HEAD),
        out_shape=jax.ShapeDtypeStruct((sequences, length, width), jnp.bfloat16),
        scratch_shapes=[
            pltpu.VMEM((length, HEAD), jnp.float32),
            pltpu.VMEM((length, HEAD), jnp.float32),
        ],
        compiler_params=params,
        cost_estimate=pl.CostEstimate(
            flops=36 * work, bytes_accessed=8 * 2**20, transcendentals=work // HEAD
        ),
    )(head_rows, grad_rows, log_totals)


def swap_pairs(count, bit):
    return [(index, index ^ bit) for index in range(count)]


def gather_group(rows):
    count = lax.axis_size("tp")
    across = lax.ppermute(rows, "tp", swap_pairs(count, 2))
    beside = lax.ppermute(rows, "tp", swap_pairs(count, 1))
    corner = lax.ppermute(across, "tp", swap_pairs(count, 1))
    return jnp.concatenate([rows, beside, across, corner], axis=0)


def scatter_group(terms):
    count = lax.axis_size("tp")
    parts = terms.reshape(count, -1, terms.shape[-1])
    first, second = (
        lax.ppermute(parts[which].astype(jnp.bfloat16), "tp", swap_pairs(count, 1)).astype(
            jnp.float32
        )
        for which in (3, 1)
    )
    passed = lax.ppermute((parts[2] + first).astype(jnp.bfloat16), "tp", swap_pairs(count, 2))
    return parts[0] + second + passed.astype(jnp.float32)


def shifted(count, step):
    return [(index, (index + step) % count) for index in range(count)]


def gather_axis(piece, name):
    count = lax.axis_size(name)
    mine = lax.axis_index(name)
    found = [piece] + [
        lax.ppermute(piece, name, shifted(count, -step)) for step in range(1, count)
    ]
    return lax.dynamic_slice_in_dim(
        jnp.stack(found + found[:-1]), (count - mine) % count, count, axis=0
    )


def gather_bit(piece, bit):
    other = lax.ppermute(piece, "tp", swap_pairs(lax.axis_size("tp"), bit))
    upper = (lax.axis_index("tp") & bit) > 0
    return jnp.where(upper, jnp.stack([other, piece]), jnp.stack([piece, other]))


def gather_dense(piece):
    fsdp_count, context_count = lax.axis_size("fsdp"), lax.axis_size("ctx")
    whole = gather_bit(gather_bit(gather_axis(gather_axis(piece, "fsdp"), "ctx"), 2), 1)
    whole = whole.reshape((2, 2, context_count, fsdp_count) + piece.shape)
    return whole.transpose(3, 2, 1, 0, 4, 5).reshape((-1,) + piece.shape)


def scatter_axis(parts, name):
    count = lax.axis_size(name)
    mine = lax.axis_index(name)
    low = parts.astype(jnp.bfloat16)
    total = lax.dynamic_index_in_dim(parts, mine, 0, keepdims=False).astype(jnp.float32)
    for step in range(1, count):
        sent = lax.dynamic_index_in_dim(low, (mine + step) % count, 0, keepdims=False)
        total = total + lax.ppermute(sent, name, shifted(count, step)).astype(jnp.float32)
    return total


def scatter_bit(parts, bit, axis):
    mine = (lax.axis_index("tp") & bit) // bit
    sent = lax.dynamic_index_in_dim(parts, 1 - mine, axis, keepdims=False).astype(jnp.bfloat16)
    kept = lax.dynamic_index_in_dim(parts, mine, axis, keepdims=False).astype(jnp.float32)
    return kept + lax.ppermute(sent, "tp", swap_pairs(lax.axis_size("tp"), bit)).astype(
        jnp.float32
    )


def scatter_dense(parts):
    fsdp_count, context_count = lax.axis_size("fsdp"), lax.axis_size("ctx")
    parts = parts.reshape((fsdp_count, context_count, 2, 2) + parts.shape[1:])
    parts = scatter_bit(scatter_bit(parts, 1, 3), 2, 2)
    return scatter_axis(scatter_axis(jnp.moveaxis(parts, 1, 0), "ctx"), "fsdp")


def hold(*refs):
    pass


def together(*values):
    spec = pl.BlockSpec(memory_space=pl.ANY)
    return pl.pallas_call(
        hold,
        in_specs=[spec] * len(values),
        out_specs=[spec] * len(values),
        out_shape=[jax.ShapeDtypeStruct(value.shape, value.dtype) for value in values],
        input_output_aliases={number: number for number in range(len(values))},
    )(*values)


def after(value, *earlier):
    spec = pl.BlockSpec(memory_space=pl.ANY)
    return pl.pallas_call(
        hold,
        in_specs=[spec] * (1 + len(earlier)),
        out_specs=spec,
        out_shape=jax.ShapeDtypeStruct(value.shape, value.dtype),
        input_output_aliases={0: 0},
    )(value, *earlier)


def per_device(
    tokens,
    routes,
    cotangent,
    norm_gains,
    query_key_value,
    attn_output,
    router_weight,
    expert_in,
    expert_out,
):
    local_seqs, local_positions, model_width = tokens.shape
    context_count = lax.axis_size("ctx")
    length = local_positions * context_count
    row_count = local_seqs * local_positions
    local_groups = KV_HEADS // context_count
    head_size = HEAD
    score_scale = HEAD ** (-0.5)
    capacity = local_positions * 3 // 8
    group_grads = by_rows(gather_group(cotangent.reshape(row_count, model_width)))
    grads_turned = by_rows(group_grads.T)
    device_count = context_count * lax.axis_size("fsdp") * lax.axis_size("tp")
    gain_count, router_count = norm_gains.size, router_weight.size
    packed = lax.all_gather(pack_rows([query_key_value, norm_gains], model_width), ALL_AXES, axis=0)
    shard_depth = expert_in.shape[2]
    chunk_experts = EXPERTS // CHUNKS
    paired = context_count == 2
    expert_shards = jnp.concatenate([expert_in, expert_out[:, None]], axis=1)
    if paired:
        last_other = lax.ppermute(
            expert_shards[EXPERTS - chunk_experts :], "ctx", swap_pairs(2, 1)
        )
        packed, last_other = together(after(packed, grads_turned), last_other)
    else:
        packed = after(packed, grads_turned)
    packed_later = gather_dense(pack_rows([attn_output, router_weight], model_width))
    inward_rows, output_rows = query_key_value.shape[0], attn_output.shape[0]
    inward_full = packed[:, :inward_rows].reshape(-1, model_width)
    gain_full = (
        packed[:, inward_rows:]
        .reshape(device_count, -1)[:, :gain_count]
        .reshape(device_count, 2, -1)
        .transpose(1, 0, 2)
        .reshape(2, model_width)
    )
    output_full = packed_later[:, :output_rows].reshape(-1, model_width)
    router_full = (
        packed_later[:, output_rows:]
        .reshape(device_count, -1)[:, :router_count]
        .reshape(device_count, EXPERTS, -1)
        .transpose(1, 0, 2)
        .reshape(EXPERTS, model_width)
    )
    my_context = lax.axis_index("ctx").astype(jnp.int32)
    if paired:
        places = jnp.stack([my_context, 1 - my_context]) * shard_depth
        steps = (2 * shard_depth, 2 * shard_depth)
    else:
        places = jnp.zeros((1,), jnp.int32)
        steps = (shard_depth,)
    expert_pieces = []
    for chunk in range(CHUNKS):
        shard = expert_shards[chunk * chunk_experts : (chunk + 1) * chunk_experts]
        if paired:
            expert_pieces.append([lax.all_gather(shard, "fsdp", axis=0)])
            if chunk == CHUNKS - 1:
                expert_pieces[chunk].append(lax.all_gather(last_other, "fsdp", axis=0))
        else:
            expert_pieces.append([lax.all_gather(shard, ("fsdp", "ctx"), axis=0)])
    gain_rows = gain_full.astype(jnp.float32)
    inputs = tokens.astype(jnp.float32).reshape(row_count, model_width)
    inverse_first = lax.rsqrt(jnp.mean(inputs * inputs, axis=1, keepdims=True) + EPS)
    normed_first = inputs * inverse_first
    first_low = (normed_first * gain_rows[0]).astype(jnp.bfloat16)
    projected = times_transposed(first_low, inward_full).reshape(
        local_seqs, local_positions, KV_HEADS, 4, head_size
    )
    positions = lax.axis_index("ctx") * local_positions + jnp.arange(
        local_positions, dtype=jnp.int32
    )
    cosine_table, sine_table = angle_tables(positions, head_size)
    cosine_rows = cosine_table[None, :, None, None, :]
    sine_rows = sine_table[None, :, None, None, :]
    turned = jnp.concatenate(
        [rotary(projected[:, :, :, :3], cosine_rows, sine_rows), projected[:, :, :, 3:]], axis=3
    )
    sent_heads = turned.astype(jnp.bfloat16).reshape(
        local_seqs, local_positions, KV_HEADS, 4 * head_size
    )
    head_rows = lax.all_to_all(sent_heads, "ctx", split_axis=2, concat_axis=1, tiled=True)
    head_rows = head_rows.reshape(local_seqs, length, -1)
    head_output, log_totals = attend(head_rows)
    head_output = head_output.reshape(local_seqs, length, local_groups, 2 * head_size)
    merged = lax.all_to_all(head_output, "ctx", split_axis=1, concat_axis=2, tiled=True).reshape(
        row_count, HEADS * head_size
    )
    hidden = inputs + times_transposed(merged, output_full)
    inverse_second = lax.rsqrt(jnp.mean(hidden * hidden, axis=1, keepdims=True) + EPS)
    normed_second = hidden * inverse_second
    second_low = (normed_second * gain_rows[1]).astype(jnp.bfloat16)
    group_rows = by_rows(gather_group(by_rows(second_low)))
    group_count = group_rows.shape[0]
    chances = jax.nn.softmax(times_transposed(group_rows, router_full), axis=-1)
    group_order = jnp.bitwise_xor(
        jnp.arange(lax.axis_size("tp"), dtype=jnp.int32), lax.axis_index("tp").astype(jnp.int32)
    )
    route_rows = jnp.take(
        routes.reshape(lax.axis_size("tp"), row_count, TOP), group_order, axis=0
    ).reshape(group_count, TOP)
    chosen_any = jnp.sum(
        (route_rows[:, :, None] == jnp.arange(EXPERTS, dtype=jnp.int32)[None, None, :]).astype(
            jnp.float32
        ),
        axis=1,
    )
    gates = jnp.pad(chances * chosen_any, ((0, 0), (0, LANES - EXPERTS)))
    group_turned = by_rows(group_rows.T)
    totals = None
    choice_total = None
    chunk_sums = []
    own_sums = []
    far_sums = []
    arrivals = []
    marks = []

    def fetch(chunk):
        near = expert_pieces[chunk][0]
        if chunk > 1:
            near = after(near, marks[chunk - 2])
            expert_pieces[chunk][0] = near
        expert_pieces[chunk].append(lax.ppermute(near, "ctx", swap_pairs(2, 1)))

    def cross(chunk):
        held = after(far_sums[chunk], marks[chunk + 1])
        arrivals.append(lax.ppermute(held, "ctx", swap_pairs(2, 1)))

    if paired:
        fetch(0)
    for chunk in range(CHUNKS):
        if paired:
            if chunk + 2 < CHUNKS:
                fetch(chunk + 1)
        moe_total, back_total, choice, *grad_pieces = expert_pass(
            places,
            steps,
            expert_pieces[chunk],
            group_rows,
            group_turned,
            group_grads,
            grads_turned,
            gates,
            totals,
            chunk * chunk_experts,
            arrivals if paired and chunk == CHUNKS - 1 else (),
        )
        totals = (moe_total, back_total)
        marks.append(choice)
        choice_total = choice if choice_total is None else choice_total + choice
        if paired:
            own_sums.append(grad_pieces[0])
            far_sums.append(grad_pieces[1])
            if chunk == 1:
                cross(0)
            elif chunk == CHUNKS - 1:
                arrivals[0] = grad_pieces[2]
        else:
            chunk_sums.append(
                lax.psum_scatter(grad_pieces[0], ("fsdp", "ctx"), scatter_dimension=0)
            )
    if paired:
        for chunk in range(1, CHUNKS - 1):
            cross(chunk)
        last_sums = [
            lax.psum_scatter(part, "fsdp", scatter_dimension=0)
            for part in (far_sums[-1], own_sums[-1])
        ]
    grad_chances = choice_total[:, :EXPERTS] * chosen_any
    grad_logits = chances * (grad_chances - jnp.sum(grad_chances * chances, axis=-1, keepdims=True))
    router_rows = router_full.astype(jnp.float32)
    grad_router = jnp.dot(grad_logits.T, group_rows.astype(jnp.float32), precision=HIGH)
    back_group = by_rows(totals[1] + jnp.dot(grad_logits, router_rows, precision=HIGH))
    grad_second = by_rows(scatter_group(back_group))
    moe_rows = by_rows(scatter_group(totals[0]))
    output = (hidden + moe_rows).astype(jnp.bfloat16).reshape(tokens.shape)
    grad_gain_second = jnp.sum(grad_second * normed_second, axis=0)
    grad_hidden = cotangent.astype(jnp.float32).reshape(row_count, model_width) + rms_back(
        grad_second, normed_second, inverse_second, gain_rows[1]
    )
    grad_attn = by_rows(grad_hidden.astype(jnp.bfloat16))
    if paired:
        grad_attn, arrivals[1] = together(grad_attn, arrivals[1])
    grad_output_weight = transposed_times(grad_attn, merged)
    grad_merged = (
        jnp.dot(grad_attn, output_full, preferred_element_type=jnp.float32)
        .astype(jnp.bfloat16)
        .reshape(local_seqs, local_positions, KV_HEADS, 2 * head_size)
    )
    grad_heads = lax.all_to_all(by_rows(grad_merged), "ctx", split_axis=2, concat_axis=1, tiled=True)
    grad_head_rows = attend(
        head_rows, grad_heads.reshape(local_seqs, length, -1), log_totals
    ).reshape(local_seqs, length, local_groups, 4 * head_size)
    if paired:
        grad_head_rows, arrivals[2] = together(grad_head_rows, arrivals[2])
        for own, arrived in zip(own_sums, arrivals):
            joined = (own.astype(jnp.float32) + arrived.astype(jnp.float32)).astype(jnp.bfloat16)
            chunk_sums.append(lax.psum_scatter(joined, "fsdp", scatter_dimension=0))
        far = lax.ppermute(last_sums[0], "ctx", swap_pairs(2, 1))
        chunk_sums.append(last_sums[1].astype(jnp.float32) + far.astype(jnp.float32))
    grad_turned = (
        lax.all_to_all(grad_head_rows, "ctx", split_axis=1, concat_axis=2, tiled=True)
        .astype(jnp.float32)
        .reshape(local_seqs, local_positions, KV_HEADS, 4, head_size)
    )
    grad_projected = (
        jnp.concatenate(
            [
                rotary_back(grad_turned[:, :, :, :3], cosine_rows, sine_rows),
                grad_turned[:, :, :, 3:],
            ],
            axis=3,
        )
        .astype(jnp.bfloat16)
        .reshape(row_count, -1)
    )
    grad_inward = transposed_times(grad_projected, first_low)
    grad_first = jnp.dot(grad_projected, inward_full, preferred_element_type=jnp.float32)
    grad_gain_first = jnp.sum(grad_first * normed_first, axis=0)
    grad_inputs = grad_hidden + rms_back(grad_first, normed_first, inverse_first, gain_rows[0])
    grad_gains = jnp.stack([grad_gain_first, grad_gain_second])

    def by_device(array, axis):
        parts = array.reshape(
            array.shape[:axis] + (device_count, -1) + array.shape[axis + 1 :]
        )
        return jnp.moveaxis(parts, axis, 0).reshape(device_count, -1)

    inward_sum = scatter_dense(
        grad_inward.astype(jnp.bfloat16).reshape((device_count,) + query_key_value.shape)
    )
    output_sum = scatter_dense(
        grad_output_weight.astype(jnp.bfloat16).reshape((device_count,) + attn_output.shape)
    )
    small = jnp.concatenate([by_device(grad_router, 1), by_device(grad_gains, 1)], axis=1)
    small_count = small.shape[1]
    small_rows = -(-small_count // (16 * LANES)) * 16
    small = jnp.pad(small, ((0, 0), (0, small_rows * LANES - small_count)))
    small_sum = scatter_dense(small.reshape(device_count, small_rows, LANES)).reshape(-1)
    expert_sums = jnp.concatenate([part.astype(jnp.float32) for part in chunk_sums], axis=0)
    return (
        output,
        grad_inputs.reshape(tokens.shape),
        small_sum[router_count:small_count].reshape(norm_gains.shape),
        inward_sum,
        output_sum,
        small_sum[:router_count].reshape(router_weight.shape),
        expert_sums[:, :2],
        expert_sums[:, 2],
    )


def solution(mesh):
    placed = (
        P(("fsdp", "tp"), "ctx", None),
        P("fsdp", "ctx", None),
        P(("fsdp", "tp"), "ctx", None),
        P(None, ("fsdp", "ctx", "tp")),
        P(("fsdp", "ctx", "tp"), None),
        P(("fsdp", "ctx", "tp"), None),
        P(None, ("fsdp", "ctx", "tp")),
        P(None, None, ("fsdp", "ctx"), "tp"),
        P(None, ("fsdp", "ctx"), "tp"),
    )
    return jax.shard_map(
        per_device,
        mesh=mesh,
        in_specs=placed,
        out_specs=(
            P(("fsdp", "tp"), "ctx", None),
            P(("fsdp", "tp"), "ctx", None),
            P(None, ("fsdp", "ctx", "tp")),
            P(("fsdp", "ctx", "tp"), None),
            P(("fsdp", "ctx", "tp"), None),
            P(None, ("fsdp", "ctx", "tp")),
            P(None, None, ("fsdp", "ctx"), "tp"),
            P(None, ("fsdp", "ctx"), "tp"),
        ),
        check_vma=False,
    )
```

```python
import functools

import jax
import jax.numpy as jnp
from jax import lax
from jax.experimental import pallas as pl
from jax.experimental.layout import Layout, with_layout_constraint
from jax.experimental.pallas import tpu as pltpu
from jax.sharding import PartitionSpec as P

HEADS = 16
KV_HEADS = 8
HEAD = 64
EXPERTS = 32
TOP = 8


EPS = 1e-06
NEG = -1e30
HIGH = lax.Precision.HIGHEST
ALL_AXES = ("fsdp", "ctx", "tp")
CHUNKS = 4
TILE = 512
LANES = 128


def times_transposed(left_side, right_side):
    return lax.dot_general(
        left_side, right_side, (((1,), (1,)), ((), ())), preferred_element_type=jnp.float32
    )


def transposed_times(left_side, right_side):
    return lax.dot_general(
        left_side, right_side, (((0,), (0,)), ((), ())), preferred_element_type=jnp.float32
    )


def angle_tables(positions, head_size):
    half_size = head_size // 2
    inverse = 10000.0 ** (-jnp.arange(half_size, dtype=jnp.float32) * 2.0 / head_size)
    angles = positions.astype(jnp.float32)[:, None] * inverse[None, :]
    return (jnp.cos(angles), jnp.sin(angles))


def rotary(values, cosine_table, sine_table):
    half_size = values.shape[-1] // 2
    former = values[..., :half_size]
    latter = values[..., half_size:]
    return jnp.concatenate(
        [former * cosine_table - latter * sine_table, latter * cosine_table + former * sine_table],
        axis=-1,
    )


def rotary_back(gradient, cosine_table, sine_table):
    half_size = gradient.shape[-1] // 2
    former = gradient[..., :half_size]
    latter = gradient[..., half_size:]
    return jnp.concatenate(
        [former * cosine_table + latter * sine_table, latter * cosine_table - former * sine_table],
        axis=-1,
    )


def rms_back(grad_normed, normed, inverse, gain_row):
    scaled_grad = grad_normed * gain_row
    return inverse * (scaled_grad - normed * jnp.mean(scaled_grad * normed, axis=1, keepdims=True))


def by_rows(array):
    return with_layout_constraint(array, Layout(tuple(range(array.ndim))))


def dot_nn(left_side, right_side):
    return lax.dot_general(
        left_side, right_side, (((1,), (0,)), ((), ())), preferred_element_type=jnp.float32
    )


def pack_rows(pieces, width):
    flat = jnp.concatenate([piece.reshape(-1) for piece in pieces])
    rows = -(-flat.shape[0] // (16 * width)) * 16
    return jnp.pad(flat, (0, rows * width - flat.shape[0])).reshape(rows, width)


def expert_kernel(first, steps, base_expert, extra, places_ref, *refs):
    count = len(steps)
    weight_refs, refs = refs[:count], refs[count:]
    rows_ref, rows_turned_ref, grad_ref, grad_turned_ref, gate_ref = refs[:5]
    refs = refs[5:]
    if not first:
        moe_in_ref, back_in_ref = refs[:2]
        refs = refs[2:]
    refs = refs[extra:]
    moe_ref, back_ref, choice_ref = refs[:3]
    out_refs, refs = refs[3 : 3 + count], refs[3 + count + extra :]
    moe, back, weight_in, weight_out, hidden_rows, grad_hidden, stage, semaphores = refs
    pair = pl.program_id(0)
    token_count = rows_ref.shape[0]
    units = weight_refs[0].shape[-1]
    depth = weight_refs[0].shape[-2]
    width = 2 * units

    last = pl.num_programs(0) - 1
    tiles = token_count // TILE

    def moves(tile, inward):
        rows = pl.ds(pl.multiple_of(tile * TILE, TILE), TILE)
        if inward:
            return (
                pltpu.make_async_copy(moe_in_ref.at[rows], moe.at[rows], semaphores.at[0, tile]),
                pltpu.make_async_copy(back_in_ref.at[rows], back.at[rows], semaphores.at[1, tile]),
            )
        return (
            pltpu.make_async_copy(moe.at[rows], moe_ref.at[rows], semaphores.at[2, tile]),
            pltpu.make_async_copy(back.at[rows], back_ref.at[rows], semaphores.at[3, tile]),
        )

    if not first:

        @pl.when(pair == 0)
        def _():
            for tile in range(tiles):
                for move in moves(tile, True):
                    move.start()

    @pl.when(pair == 0)
    def _():
        choice_ref[...] = jnp.zeros_like(choice_ref)
        if first:
            moe[...] = jnp.zeros_like(moe)
            back[...] = jnp.zeros_like(back)

    def place(number, block):
        return pl.ds(
            pl.multiple_of(places_ref[number] + block * steps[number], depth), depth
        )

    for number, ref in enumerate(weight_refs):
        for block in range(ref.shape[0]):
            where = place(number, block)
            for which in range(2):
                columns = slice(which * units, (which + 1) * units)
                weight_in[where, columns] = ref[block, which, 0]
                weight_in[where, width + which * units : width + (which + 1) * units] = ref[
                    block, which, 1
                ]
                weight_out[where, columns] = ref[block, which, 2]

    expert = base_expert + 2 * pair

    def tile_step(tile, carry):
        rows = pl.ds(pl.multiple_of(tile * TILE, TILE), TILE)
        both = dot_nn(rows_ref[rows, :], weight_in[...])
        probe = dot_nn(grad_ref[rows, :], weight_out[...])
        gates = gate_ref[rows, :]
        lane = lax.broadcasted_iota(jnp.int32, gates.shape, 1)
        pre_gate = both[:, :width]
        pre_up = both[:, width:]
        gate = jnp.concatenate(
            [
                jnp.broadcast_to(
                    jnp.sum(
                        jnp.where(lane == expert + which, gates, 0.0), axis=1, keepdims=True
                    ),
                    (TILE, units),
                )
                for which in range(2)
            ],
            axis=1,
        )
        sigmoid_gate = 1.0 / (1.0 + jnp.exp(-pre_gate))
        swish_gate = pre_gate * sigmoid_gate
        hidden = (swish_gate * pre_up).astype(jnp.bfloat16).astype(jnp.float32)
        gated = (hidden * gate).astype(jnp.bfloat16)
        product = probe * hidden
        choice = choice_ref[rows, :]
        for which in range(2):
            total = jnp.sum(
                product[:, which * units : (which + 1) * units], axis=1, keepdims=True
            )
            choice = jnp.where(lane == expert + which, total, choice)
        choice_ref[rows, :] = choice
        scaled = probe * gate
        grad_gate = (
            scaled * pre_up * sigmoid_gate * (1.0 + pre_gate * (1.0 - sigmoid_gate))
        ).astype(jnp.bfloat16)
        grad_up = (scaled * swish_gate).astype(jnp.bfloat16)
        hidden_rows[rows, :] = gated
        grad_hidden[rows, :width] = grad_gate
        grad_hidden[rows, width:] = grad_up
        if not first:

            @pl.when(pair == 0)
            def _():
                for move in moves(tile, True):
                    move.wait()

        moe[rows, :] += times_transposed(gated, weight_out[...])
        back[rows, :] += times_transposed(
            jnp.concatenate([grad_gate, grad_up], axis=1), weight_in[...]
        )

        @pl.when(pair == last)
        def _():
            for move in moves(tile, False):
                move.start()

        return carry

    lax.fori_loop(0, tiles, tile_step, 0, unroll=True)

    slab = 512

    def weight_step(tile, carry):
        rows = pl.ds(pl.multiple_of(tile * slab, slab), slab)
        stage[rows, : 2 * width] = dot_nn(rows_turned_ref[rows, :], grad_hidden[...]).astype(
            jnp.bfloat16
        )
        stage[rows, 2 * width :] = dot_nn(grad_turned_ref[rows, :], hidden_rows[...]).astype(
            jnp.bfloat16
        )
        return carry

    lax.fori_loop(0, rows_turned_ref.shape[0] // slab, weight_step, 0)

    for number, ref in enumerate(out_refs):
        for block in range(ref.shape[0]):
            where = place(number, block)
            for which in range(2):
                for kind in range(3):
                    start = kind * width + which * units
                    ref[block, which, kind] = stage[where, start : start + units]

    @pl.when(pair == last)
    def _():
        for tile in range(tiles):
            for move in moves(tile, False):
                move.wait()


def expert_pass(
    places, steps, weights, rows, rows_turned, grads, grads_turned, gates, totals, base_expert, earlier=()
):
    first = totals is None
    token_count, model_width = rows.shape
    experts, _, depth, units = weights[0].shape[1:]

    def whole(array):
        return pl.BlockSpec(
            array.shape, lambda *_: (0,) * array.ndim, pipeline_mode=pl.Buffered(1)
        )

    weight_specs = [
        pl.BlockSpec((piece.shape[0], 2, 3, depth, units), lambda pair, _: (0, pair, 0, 0, 0))
        for piece in weights
    ]
    operands = [*weights, rows, rows_turned, grads, grads_turned, gates]
    specs = [*weight_specs, *(whole(array) for array in operands[len(weights) :])]
    aliases = {}
    if not first:
        aliases = {1 + len(operands): 0, 2 + len(operands): 1}
        operands += list(totals)
        specs += [pl.BlockSpec(memory_space=pl.ANY)] * 2
    for number, array in enumerate(earlier):
        aliases[1 + len(operands)] = 3 + len(weights) + number
        operands.append(array)
        specs.append(pl.BlockSpec(memory_space=pl.ANY))
    total_shape = jax.ShapeDtypeStruct((token_count, model_width), jnp.float32)
    products = 2 * token_count * model_width * units * experts
    return pl.pallas_call(
        functools.partial(expert_kernel, first, steps, base_expert, len(earlier)),
        grid_spec=pltpu.PrefetchScalarGridSpec(
            num_scalar_prefetch=1,
            grid=(experts // 2,),
            in_specs=specs,
            out_specs=[
                pl.BlockSpec(memory_space=pl.ANY),
                pl.BlockSpec(memory_space=pl.ANY),
                pl.BlockSpec((token_count, LANES), lambda *_: (0, 0)),
                *weight_specs,
                *([pl.BlockSpec(memory_space=pl.ANY)] * len(earlier)),
            ],
            scratch_shapes=[
                pltpu.VMEM((token_count, model_width), jnp.float32),
                pltpu.VMEM((token_count, model_width), jnp.float32),
                pltpu.VMEM((model_width, 4 * units), jnp.bfloat16),
                pltpu.VMEM((model_width, 2 * units), jnp.bfloat16),
                pltpu.VMEM((token_count, 2 * units), jnp.bfloat16),
                pltpu.VMEM((token_count, 4 * units), jnp.bfloat16),
                pltpu.VMEM((model_width, 6 * units), jnp.bfloat16),
                pltpu.SemaphoreType.DMA((4, token_count // TILE)),
            ],
        ),
        out_shape=[
            total_shape,
            total_shape,
            jax.ShapeDtypeStruct((token_count, LANES), jnp.float32),
            *(jax.ShapeDtypeStruct(piece.shape, jnp.bfloat16) for piece in weights),
            *(jax.ShapeDtypeStruct(array.shape, array.dtype) for array in earlier),
        ],
        input_output_aliases=aliases,
        compiler_params=pltpu.CompilerParams(
            dimension_semantics=("arbitrary",), vmem_limit_bytes=60 * 2**20
        ),
        cost_estimate=pl.CostEstimate(
            flops=9 * products,
            bytes_accessed=40 * 2**20,
            transcendentals=token_count * units * experts,
        ),
    )(places, *operands)


def visible_mask(first_row, first_key, row_count, key_count):
    rows = first_row + lax.broadcasted_iota(jnp.int32, (row_count, key_count), 0)
    keys = first_key + lax.broadcasted_iota(jnp.int32, (row_count, key_count), 1)
    return rows >= keys


def attend_kernel(block, heads_ref, out_ref, log_ref):
    length = heads_ref.shape[1]
    keys = heads_ref[0, :, 2 * HEAD : 3 * HEAD]
    values = heads_ref[0, :, 3 * HEAD :]
    for offset in range(0, length, block):
        limit = offset + block
        mask = visible_mask(offset, 0, block, limit)
        for which in range(2):
            lanes = slice(which * HEAD, (which + 1) * HEAD)
            query = heads_ref[0, offset:limit, lanes]
            scores = times_transposed(query, keys[:limit]) * HEAD ** (-0.5)
            scores = jnp.where(mask, scores, NEG)
            top_score = jnp.max(scores, axis=1, keepdims=True)
            exponent = jnp.exp(scores - top_score)
            denominator = jnp.sum(exponent, axis=1, keepdims=True)
            weights = (exponent * (1.0 / denominator)).astype(jnp.bfloat16)
            out_ref[0, offset:limit, lanes] = dot_nn(weights, values[:limit]).astype(jnp.bfloat16)
            log_ref[0, 0, offset:limit, which : which + 1] = top_score + jnp.log(denominator)


def attend_back_kernel(block, heads_ref, grad_ref, log_ref, out_ref, grad_keys, grad_values):
    length = heads_ref.shape[1]
    grad_keys[...] = jnp.zeros_like(grad_keys)
    grad_values[...] = jnp.zeros_like(grad_values)
    keys = heads_ref[0, :, 2 * HEAD : 3 * HEAD]
    values = heads_ref[0, :, 3 * HEAD :]
    for offset in range(0, length, block):
        limit = offset + block
        mask = visible_mask(offset, 0, block, limit)
        for which in range(2):
            lanes = slice(which * HEAD, (which + 1) * HEAD)
            query = heads_ref[0, offset:limit, lanes]
            grad = grad_ref[0, offset:limit, lanes]
            scores = times_transposed(query, keys[:limit]) * HEAD ** (-0.5)
            log_total = log_ref[0, 0, offset:limit, which : which + 1]
            weights = jnp.where(mask, jnp.exp(jnp.where(mask, scores, NEG) - log_total), 0.0)
            grad_weights = times_transposed(grad, values[:limit])
            middle = jnp.sum(weights * grad_weights, axis=1, keepdims=True)
            grad_scores = (weights * (grad_weights - middle)).astype(jnp.bfloat16)
            grad_values[:limit, :] += transposed_times(weights.astype(jnp.bfloat16), grad)
            grad_keys[:limit, :] += transposed_times(grad_scores, query)
            out_ref[0, offset:limit, lanes] = (
                dot_nn(grad_scores, keys[:limit]) * HEAD ** (-0.5)
            ).astype(jnp.bfloat16)
    out_ref[0, :, 2 * HEAD : 3 * HEAD] = (grad_keys[...] * HEAD ** (-0.5)).astype(jnp.bfloat16)
    out_ref[0, :, 3 * HEAD :] = grad_values[...].astype(jnp.bfloat16)


def attend(head_rows, grad_rows=None, log_totals=None):
    sequences, length, width = head_rows.shape
    groups = width // (4 * HEAD)
    block = min(256, length)

    def per_group(lane_count):
        return pl.BlockSpec((1, length, lane_count), lambda s, g: (s, 0, g))

    logs = pl.BlockSpec((1, 1, length, 2), lambda s, g: (s, g, 0, 0))
    work = sequences * groups * length * length * HEAD * 2
    params = pltpu.CompilerParams(
        dimension_semantics=("arbitrary", "arbitrary"), vmem_limit_bytes=48 * 2**20
    )
    if grad_rows is None:
        return pl.pallas_call(
            functools.partial(attend_kernel, block),
            grid=(sequences, groups),
            in_specs=[per_group(4 * HEAD)],
            out_specs=[per_group(2 * HEAD), logs],
            out_shape=[
                jax.ShapeDtypeStruct((sequences, length, groups * 2 * HEAD), jnp.bfloat16),
                jax.ShapeDtypeStruct((sequences, groups, length, 2), jnp.float32),
            ],
            compiler_params=params,
            cost_estimate=pl.CostEstimate(
                flops=16 * work, bytes_accessed=8 * 2**20, transcendentals=work // HEAD
            ),
        )(head_rows)
    return pl.pallas_call(
        functools.partial(attend_back_kernel, block),
        grid=(sequences, groups),
        in_specs=[per_group(4 * HEAD), per_group(2 * HEAD), logs],
        out_specs=per_group(4 * HEAD),
        out_shape=jax.ShapeDtypeStruct((sequences, length, width), jnp.bfloat16),
        scratch_shapes=[
            pltpu.VMEM((length, HEAD), jnp.float32),
            pltpu.VMEM((length, HEAD), jnp.float32),
        ],
        compiler_params=params,
        cost_estimate=pl.CostEstimate(
            flops=36 * work, bytes_accessed=8 * 2**20, transcendentals=work // HEAD
        ),
    )(head_rows, grad_rows, log_totals)


def swap_pairs(count, bit):
    return [(index, index ^ bit) for index in range(count)]


def gather_group(rows):
    count = lax.axis_size("tp")
    across = lax.ppermute(rows, "tp", swap_pairs(count, 2))
    beside = lax.ppermute(rows, "tp", swap_pairs(count, 1))
    corner = lax.ppermute(across, "tp", swap_pairs(count, 1))
    return jnp.concatenate([rows, beside, across, corner], axis=0)


def scatter_group(terms):
    count = lax.axis_size("tp")
    parts = terms.reshape(count, -1, terms.shape[-1])
    first, second = (
        lax.ppermute(parts[which].astype(jnp.bfloat16), "tp", swap_pairs(count, 1)).astype(
            jnp.float32
        )
        for which in (3, 1)
    )
    passed = lax.ppermute((parts[2] + first).astype(jnp.bfloat16), "tp", swap_pairs(count, 2))
    return parts[0] + second + passed.astype(jnp.float32)


def shifted(count, step):
    return [(index, (index + step) % count) for index in range(count)]


def gather_axis(piece, name):
    count = lax.axis_size(name)
    mine = lax.axis_index(name)
    found = [piece] + [
        lax.ppermute(piece, name, shifted(count, -step)) for step in range(1, count)
    ]
    return lax.dynamic_slice_in_dim(
        jnp.stack(found + found[:-1]), (count - mine) % count, count, axis=0
    )


def gather_bit(piece, bit):
    other = lax.ppermute(piece, "tp", swap_pairs(lax.axis_size("tp"), bit))
    upper = (lax.axis_index("tp") & bit) > 0
    return jnp.where(upper, jnp.stack([other, piece]), jnp.stack([piece, other]))


def gather_dense(piece):
    fsdp_count, context_count = lax.axis_size("fsdp"), lax.axis_size("ctx")
    whole = gather_bit(gather_bit(gather_axis(gather_axis(piece, "fsdp"), "ctx"), 2), 1)
    whole = whole.reshape((2, 2, context_count, fsdp_count) + piece.shape)
    return whole.transpose(3, 2, 1, 0, 4, 5).reshape((-1,) + piece.shape)


def scatter_axis(parts, name):
    count = lax.axis_size(name)
    mine = lax.axis_index(name)
    low = parts.astype(jnp.bfloat16)
    total = lax.dynamic_index_in_dim(parts, mine, 0, keepdims=False).astype(jnp.float32)
    for step in range(1, count):
        sent = lax.dynamic_index_in_dim(low, (mine + step) % count, 0, keepdims=False)
        total = total + lax.ppermute(sent, name, shifted(count, step)).astype(jnp.float32)
    return total


def scatter_bit(parts, bit, axis):
    mine = (lax.axis_index("tp") & bit) // bit
    sent = lax.dynamic_index_in_dim(parts, 1 - mine, axis, keepdims=False).astype(jnp.bfloat16)
    kept = lax.dynamic_index_in_dim(parts, mine, axis, keepdims=False).astype(jnp.float32)
    return kept + lax.ppermute(sent, "tp", swap_pairs(lax.axis_size("tp"), bit)).astype(
        jnp.float32
    )


def scatter_dense(parts):
    fsdp_count, context_count = lax.axis_size("fsdp"), lax.axis_size("ctx")
    parts = parts.reshape((fsdp_count, context_count, 2, 2) + parts.shape[1:])
    parts = scatter_bit(scatter_bit(parts, 1, 3), 2, 2)
    return scatter_axis(scatter_axis(jnp.moveaxis(parts, 1, 0), "ctx"), "fsdp")


def hold(*refs):
    pass


def together(*values):
    spec = pl.BlockSpec(memory_space=pl.ANY)
    return pl.pallas_call(
        hold,
        in_specs=[spec] * len(values),
        out_specs=[spec] * len(values),
        out_shape=[jax.ShapeDtypeStruct(value.shape, value.dtype) for value in values],
        input_output_aliases={number: number for number in range(len(values))},
    )(*values)


def after(value, *earlier):
    spec = pl.BlockSpec(memory_space=pl.ANY)
    return pl.pallas_call(
        hold,
        in_specs=[spec] * (1 + len(earlier)),
        out_specs=spec,
        out_shape=jax.ShapeDtypeStruct(value.shape, value.dtype),
        input_output_aliases={0: 0},
    )(value, *earlier)


def per_device(
    tokens,
    routes,
    cotangent,
    norm_gains,
    query_key_value,
    attn_output,
    router_weight,
    expert_in,
    expert_out,
):
    local_seqs, local_positions, model_width = tokens.shape
    context_count = lax.axis_size("ctx")
    length = local_positions * context_count
    row_count = local_seqs * local_positions
    local_groups = KV_HEADS // context_count
    head_size = HEAD
    score_scale = HEAD ** (-0.5)
    capacity = local_positions * 3 // 8
    group_grads = by_rows(gather_group(cotangent.reshape(row_count, model_width)))
    grads_turned = by_rows(group_grads.T)
    device_count = context_count * lax.axis_size("fsdp") * lax.axis_size("tp")
    gain_count, router_count = norm_gains.size, router_weight.size
    packed = lax.all_gather(pack_rows([query_key_value, norm_gains], model_width), ALL_AXES, axis=0)
    shard_depth = expert_in.shape[2]
    chunk_experts = EXPERTS // CHUNKS
    paired = context_count == 2
    expert_shards = jnp.concatenate([expert_in, expert_out[:, None]], axis=1)
    if paired:
        last_other = lax.ppermute(
            expert_shards[EXPERTS - chunk_experts :], "ctx", swap_pairs(2, 1)
        )
        packed, last_other = together(after(packed, grads_turned), last_other)
    else:
        packed = after(packed, grads_turned)
    packed_later = gather_dense(pack_rows([attn_output, router_weight], model_width))
    inward_rows, output_rows = query_key_value.shape[0], attn_output.shape[0]
    inward_full = packed[:, :inward_rows].reshape(-1, model_width)
    gain_full = (
        packed[:, inward_rows:]
        .reshape(device_count, -1)[:, :gain_count]
        .reshape(device_count, 2, -1)
        .transpose(1, 0, 2)
        .reshape(2, model_width)
    )
    output_full = packed_later[:, :output_rows].reshape(-1, model_width)
    router_full = (
        packed_later[:, output_rows:]
        .reshape(device_count, -1)[:, :router_count]
        .reshape(device_count, EXPERTS, -1)
        .transpose(1, 0, 2)
        .reshape(EXPERTS, model_width)
    )
    my_context = lax.axis_index("ctx").astype(jnp.int32)
    if paired:
        places = jnp.stack([my_context, 1 - my_context]) * shard_depth
        steps = (2 * shard_depth, 2 * shard_depth)
    else:
        places = jnp.zeros((1,), jnp.int32)
        steps = (shard_depth,)
    expert_pieces = []
    for chunk in range(CHUNKS):
        shard = expert_shards[chunk * chunk_experts : (chunk + 1) * chunk_experts]
        if paired:
            expert_pieces.append([lax.all_gather(shard, "fsdp", axis=0)])
            if chunk == CHUNKS - 1:
                expert_pieces[chunk].append(lax.all_gather(last_other, "fsdp", axis=0))
        else:
            expert_pieces.append([lax.all_gather(shard, ("fsdp", "ctx"), axis=0)])
    gain_rows = gain_full.astype(jnp.float32)
    inputs = tokens.astype(jnp.float32).reshape(row_count, model_width)
    inverse_first = lax.rsqrt(jnp.mean(inputs * inputs, axis=1, keepdims=True) + EPS)
    normed_first = inputs * inverse_first
    first_low = (normed_first * gain_rows[0]).astype(jnp.bfloat16)
    projected = times_transposed(first_low, inward_full).reshape(
        local_seqs, local_positions, KV_HEADS, 4, head_size
    )
    positions = lax.axis_index("ctx") * local_positions + jnp.arange(
        local_positions, dtype=jnp.int32
    )
    cosine_table, sine_table = angle_tables(positions, head_size)
    cosine_rows = cosine_table[None, :, None, None, :]
    sine_rows = sine_table[None, :, None, None, :]
    turned = jnp.concatenate(
        [rotary(projected[:, :, :, :3], cosine_rows, sine_rows), projected[:, :, :, 3:]], axis=3
    )
    sent_heads = turned.astype(jnp.bfloat16).reshape(
        local_seqs, local_positions, KV_HEADS, 4 * head_size
    )
    head_rows = lax.all_to_all(sent_heads, "ctx", split_axis=2, concat_axis=1, tiled=True)
    head_rows = head_rows.reshape(local_seqs, length, -1)
    head_output, log_totals = attend(head_rows)
    head_output = head_output.reshape(local_seqs, length, local_groups, 2 * head_size)
    merged = lax.all_to_all(head_output, "ctx", split_axis=1, concat_axis=2, tiled=True).reshape(
        row_count, HEADS * head_size
    )
    hidden = inputs + times_transposed(merged, output_full)
    inverse_second = lax.rsqrt(jnp.mean(hidden * hidden, axis=1, keepdims=True) + EPS)
    normed_second = hidden * inverse_second
    second_low = (normed_second * gain_rows[1]).astype(jnp.bfloat16)
    group_rows = by_rows(gather_group(by_rows(second_low)))
    group_count = group_rows.shape[0]
    chances = jax.nn.softmax(times_transposed(group_rows, router_full), axis=-1)
    group_order = jnp.bitwise_xor(
        jnp.arange(lax.axis_size("tp"), dtype=jnp.int32), lax.axis_index("tp").astype(jnp.int32)
    )
    route_rows = jnp.take(
        routes.reshape(lax.axis_size("tp"), row_count, TOP), group_order, axis=0
    ).reshape(group_count, TOP)
    chosen_any = jnp.sum(
        (route_rows[:, :, None] == jnp.arange(EXPERTS, dtype=jnp.int32)[None, None, :]).astype(
            jnp.float32
        ),
        axis=1,
    )
    gates = jnp.pad(chances * chosen_any, ((0, 0), (0, LANES - EXPERTS)))
    group_turned = by_rows(group_rows.T)
    totals = None
    choice_total = None
    chunk_sums = []
    own_sums = []
    far_sums = []
    arrivals = []
    marks = []

    def fetch(chunk):
        near = expert_pieces[chunk][0]
        if chunk > 1:
            near = after(near, marks[chunk - 2])
            expert_pieces[chunk][0] = near
        expert_pieces[chunk].append(lax.ppermute(near, "ctx", swap_pairs(2, 1)))

    def cross(chunk):
        held = after(far_sums[chunk], marks[chunk + 1]) if chunk > 1 else far_sums[chunk]
        arrivals.append(lax.ppermute(held, "ctx", swap_pairs(2, 1)))

    if paired:
        fetch(0)
    for chunk in range(CHUNKS):
        if paired:
            if chunk + 2 < CHUNKS:
                fetch(chunk + 1)
        moe_total, back_total, choice, *grad_pieces = expert_pass(
            places,
            steps,
            expert_pieces[chunk],
            group_rows,
            group_turned,
            group_grads,
            grads_turned,
            gates,
            totals,
            chunk * chunk_experts,
            arrivals if paired and chunk == CHUNKS - 1 else (),
        )
        totals = (moe_total, back_total)
        marks.append(choice)
        choice_total = choice if choice_total is None else choice_total + choice
        if paired:
            own_sums.append(grad_pieces[0])
            far_sums.append(grad_pieces[1])
            if chunk == 1:
                cross(1)
            elif chunk == CHUNKS - 1:
                arrivals[0] = grad_pieces[2]
        else:
            chunk_sums.append(
                lax.psum_scatter(grad_pieces[0], ("fsdp", "ctx"), scatter_dimension=0)
            )
    if paired:
        cross(2)
        first_sums, last_sums = (
            [
                by_rows(lax.psum_scatter(part, "fsdp", scatter_dimension=0))
                for part in (far_sums[chunk], own_sums[chunk])
            ]
            for chunk in (0, CHUNKS - 1)
        )
    grad_chances = choice_total[:, :EXPERTS] * chosen_any
    grad_logits = chances * (grad_chances - jnp.sum(grad_chances * chances, axis=-1, keepdims=True))
    router_rows = router_full.astype(jnp.float32)
    grad_router = jnp.dot(grad_logits.T, group_rows.astype(jnp.float32), precision=HIGH)
    back_group = by_rows(totals[1] + jnp.dot(grad_logits, router_rows, precision=HIGH))
    if paired:
        back_group, *first_sums = together(back_group, *first_sums)
    grad_second = by_rows(scatter_group(back_group))
    grad_gain_second = jnp.sum(grad_second * normed_second, axis=0)
    grad_hidden = cotangent.astype(jnp.float32).reshape(row_count, model_width) + rms_back(
        grad_second, normed_second, inverse_second, gain_rows[1]
    )
    grad_attn = by_rows(grad_hidden.astype(jnp.bfloat16))
    if paired:
        grad_attn, arrivals[1] = together(grad_attn, arrivals[1])
    moe_rows = by_rows(scatter_group(after(totals[0], grad_attn)))
    output = (hidden + moe_rows).astype(jnp.bfloat16).reshape(tokens.shape)
    grad_output_weight = transposed_times(grad_attn, merged)
    grad_merged = (
        jnp.dot(grad_attn, output_full, preferred_element_type=jnp.float32)
        .astype(jnp.bfloat16)
        .reshape(local_seqs, local_positions, KV_HEADS, 2 * head_size)
    )
    grad_heads = lax.all_to_all(by_rows(grad_merged), "ctx", split_axis=2, concat_axis=1, tiled=True)
    grad_head_rows = attend(
        head_rows, grad_heads.reshape(local_seqs, length, -1), log_totals
    ).reshape(local_seqs, length, local_groups, 4 * head_size)
    if paired:
        for own, arrived in zip(own_sums[1:-1], arrivals):
            joined = (own.astype(jnp.float32) + arrived.astype(jnp.float32)).astype(jnp.bfloat16)
            chunk_sums.append(lax.psum_scatter(joined, "fsdp", scatter_dimension=0))
        for far, own in (first_sums, last_sums):
            far = lax.ppermute(far, "ctx", swap_pairs(2, 1))
            chunk_sums.append(own.astype(jnp.float32) + far.astype(jnp.float32))
        chunk_sums = [chunk_sums[2], chunk_sums[0], chunk_sums[1], chunk_sums[3]]
    grad_turned = (
        lax.all_to_all(grad_head_rows, "ctx", split_axis=1, concat_axis=2, tiled=True)
        .astype(jnp.float32)
        .reshape(local_seqs, local_positions, KV_HEADS, 4, head_size)
    )
    grad_projected = (
        jnp.concatenate(
            [
                rotary_back(grad_turned[:, :, :, :3], cosine_rows, sine_rows),
                grad_turned[:, :, :, 3:],
            ],
            axis=3,
        )
        .astype(jnp.bfloat16)
        .reshape(row_count, -1)
    )
    grad_inward = transposed_times(grad_projected, first_low)
    grad_first = jnp.dot(grad_projected, inward_full, preferred_element_type=jnp.float32)
    grad_gain_first = jnp.sum(grad_first * normed_first, axis=0)
    grad_inputs = grad_hidden + rms_back(grad_first, normed_first, inverse_first, gain_rows[0])
    grad_gains = jnp.stack([grad_gain_first, grad_gain_second])

    def by_device(array, axis):
        parts = array.reshape(
            array.shape[:axis] + (device_count, -1) + array.shape[axis + 1 :]
        )
        return jnp.moveaxis(parts, axis, 0).reshape(device_count, -1)

    inward_sum = scatter_dense(
        grad_inward.astype(jnp.bfloat16).reshape((device_count,) + query_key_value.shape)
    )
    output_sum = scatter_dense(
        grad_output_weight.astype(jnp.bfloat16).reshape((device_count,) + attn_output.shape)
    )
    small = jnp.concatenate([by_device(grad_router, 1), by_device(grad_gains, 1)], axis=1)
    small_count = small.shape[1]
    small_rows = -(-small_count // (16 * LANES)) * 16
    small = jnp.pad(small, ((0, 0), (0, small_rows * LANES - small_count)))
    small_sum = scatter_dense(small.reshape(device_count, small_rows, LANES)).reshape(-1)
    return (
        output,
        grad_inputs.reshape(tokens.shape),
        small_sum[router_count:small_count].reshape(norm_gains.shape),
        inward_sum,
        output_sum,
        small_sum[:router_count].reshape(router_weight.shape),
        jnp.concatenate([part[:, :2].astype(jnp.float32) for part in chunk_sums], axis=0),
        jnp.concatenate([part[:, 2].astype(jnp.float32) for part in chunk_sums], axis=0),
    )


def solution(mesh):
    placed = (
        P(("fsdp", "tp"), "ctx", None),
        P("fsdp", "ctx", None),
        P(("fsdp", "tp"), "ctx", None),
        P(None, ("fsdp", "ctx", "tp")),
        P(("fsdp", "ctx", "tp"), None),
        P(("fsdp", "ctx", "tp"), None),
        P(None, ("fsdp", "ctx", "tp")),
        P(None, None, ("fsdp", "ctx"), "tp"),
        P(None, ("fsdp", "ctx"), "tp"),
    )
    return jax.shard_map(
        per_device,
        mesh=mesh,
        in_specs=placed,
        out_specs=(
            P(("fsdp", "tp"), "ctx", None),
            P(("fsdp", "tp"), "ctx", None),
            P(None, ("fsdp", "ctx", "tp")),
            P(("fsdp", "ctx", "tp"), None),
            P(("fsdp", "ctx", "tp"), None),
            P(None, ("fsdp", "ctx", "tp")),
            P(None, None, ("fsdp", "ctx"), "tp"),
            P(None, ("fsdp", "ctx"), "tp"),
        ),
        check_vma=False,
    )
```

```python
import functools

import jax
import jax.numpy as jnp
from jax import lax
from jax.experimental import pallas as pl
from jax.experimental.layout import Layout, with_layout_constraint
from jax.experimental.pallas import tpu as pltpu
from jax.sharding import PartitionSpec as P

HEADS = 16
KV_HEADS = 8
HEAD = 64
EXPERTS = 32
TOP = 8


EPS = 1e-06
NEG = -1e30
HIGH = lax.Precision.HIGHEST
ALL_AXES = ("fsdp", "ctx", "tp")
CHUNKS = 4
TILE = 512
LANES = 128


def times_transposed(left_side, right_side):
    return lax.dot_general(
        left_side, right_side, (((1,), (1,)), ((), ())), preferred_element_type=jnp.float32
    )


def transposed_times(left_side, right_side):
    return lax.dot_general(
        left_side, right_side, (((0,), (0,)), ((), ())), preferred_element_type=jnp.float32
    )


def angle_tables(positions, head_size):
    half_size = head_size // 2
    inverse = 10000.0 ** (-jnp.arange(half_size, dtype=jnp.float32) * 2.0 / head_size)
    angles = positions.astype(jnp.float32)[:, None] * inverse[None, :]
    return (jnp.cos(angles), jnp.sin(angles))


def rotary(values, cosine_table, sine_table):
    half_size = values.shape[-1] // 2
    former = values[..., :half_size]
    latter = values[..., half_size:]
    return jnp.concatenate(
        [former * cosine_table - latter * sine_table, latter * cosine_table + former * sine_table],
        axis=-1,
    )


def rotary_back(gradient, cosine_table, sine_table):
    half_size = gradient.shape[-1] // 2
    former = gradient[..., :half_size]
    latter = gradient[..., half_size:]
    return jnp.concatenate(
        [former * cosine_table + latter * sine_table, latter * cosine_table - former * sine_table],
        axis=-1,
    )


def rms_back(grad_normed, normed, inverse, gain_row):
    scaled_grad = grad_normed * gain_row
    return inverse * (scaled_grad - normed * jnp.mean(scaled_grad * normed, axis=1, keepdims=True))


def by_rows(array):
    return with_layout_constraint(array, Layout(tuple(range(array.ndim))))


def dot_nn(left_side, right_side):
    return lax.dot_general(
        left_side, right_side, (((1,), (0,)), ((), ())), preferred_element_type=jnp.float32
    )


def pack_rows(pieces, width):
    flat = jnp.concatenate([piece.reshape(-1) for piece in pieces])
    rows = -(-flat.shape[0] // (16 * width)) * 16
    return jnp.pad(flat, (0, rows * width - flat.shape[0])).reshape(rows, width)


def expert_kernel(first, steps, base_expert, extra, places_ref, *refs):
    count = len(steps)
    weight_refs, refs = refs[:count], refs[count:]
    rows_ref, rows_turned_ref, grad_ref, grad_turned_ref, gate_ref = refs[:5]
    refs = refs[5:]
    if not first:
        moe_in_ref, back_in_ref = refs[:2]
        refs = refs[2:]
    refs = refs[extra:]
    moe_ref, back_ref, choice_ref = refs[:3]
    out_refs, refs = refs[3 : 3 + count], refs[3 + count + extra :]
    moe, back, weight_in, weight_out, hidden_rows, grad_hidden, stage, semaphores = refs
    pair = pl.program_id(0)
    token_count = rows_ref.shape[0]
    units = weight_refs[0].shape[-1]
    depth = weight_refs[0].shape[-2]
    width = 2 * units

    last = pl.num_programs(0) - 1
    tiles = token_count // TILE

    def moves(tile, inward):
        rows = pl.ds(pl.multiple_of(tile * TILE, TILE), TILE)
        if inward:
            return (
                pltpu.make_async_copy(moe_in_ref.at[rows], moe.at[rows], semaphores.at[0, tile]),
                pltpu.make_async_copy(back_in_ref.at[rows], back.at[rows], semaphores.at[1, tile]),
            )
        return (
            pltpu.make_async_copy(moe.at[rows], moe_ref.at[rows], semaphores.at[2, tile]),
            pltpu.make_async_copy(back.at[rows], back_ref.at[rows], semaphores.at[3, tile]),
        )

    if not first:

        @pl.when(pair == 0)
        def _():
            for tile in range(tiles):
                for move in moves(tile, True):
                    move.start()

    @pl.when(pair == 0)
    def _():
        choice_ref[...] = jnp.zeros_like(choice_ref)
        if first:
            moe[...] = jnp.zeros_like(moe)
            back[...] = jnp.zeros_like(back)

    def place(number, block):
        return pl.ds(
            pl.multiple_of(places_ref[number] + block * steps[number], depth), depth
        )

    for number, ref in enumerate(weight_refs):
        for block in range(ref.shape[0]):
            where = place(number, block)
            for which in range(2):
                columns = slice(which * units, (which + 1) * units)
                weight_in[where, columns] = ref[block, which, 0]
                weight_in[where, width + which * units : width + (which + 1) * units] = ref[
                    block, which, 1
                ]
                weight_out[where, columns] = ref[block, which, 2]

    expert = base_expert + 2 * pair

    def tile_step(tile, carry):
        rows = pl.ds(pl.multiple_of(tile * TILE, TILE), TILE)
        both = dot_nn(rows_ref[rows, :], weight_in[...])
        probe = dot_nn(grad_ref[rows, :], weight_out[...])
        gates = gate_ref[rows, :]
        lane = lax.broadcasted_iota(jnp.int32, gates.shape, 1)
        pre_gate = both[:, :width]
        pre_up = both[:, width:]
        gate = jnp.concatenate(
            [
                jnp.broadcast_to(
                    jnp.sum(
                        jnp.where(lane == expert + which, gates, 0.0), axis=1, keepdims=True
                    ),
                    (TILE, units),
                )
                for which in range(2)
            ],
            axis=1,
        )
        sigmoid_gate = 1.0 / (1.0 + jnp.exp(-pre_gate))
        swish_gate = pre_gate * sigmoid_gate
        hidden = (swish_gate * pre_up).astype(jnp.bfloat16).astype(jnp.float32)
        gated = (hidden * gate).astype(jnp.bfloat16)
        product = probe * hidden
        choice = choice_ref[rows, :]
        for which in range(2):
            total = jnp.sum(
                product[:, which * units : (which + 1) * units], axis=1, keepdims=True
            )
            choice = jnp.where(lane == expert + which, total, choice)
        choice_ref[rows, :] = choice
        scaled = probe * gate
        grad_gate = (
            scaled * pre_up * sigmoid_gate * (1.0 + pre_gate * (1.0 - sigmoid_gate))
        ).astype(jnp.bfloat16)
        grad_up = (scaled * swish_gate).astype(jnp.bfloat16)
        hidden_rows[rows, :] = gated
        grad_hidden[rows, :width] = grad_gate
        grad_hidden[rows, width:] = grad_up
        if not first:

            @pl.when(pair == 0)
            def _():
                for move in moves(tile, True):
                    move.wait()

        moe[rows, :] += times_transposed(gated, weight_out[...])
        back[rows, :] += times_transposed(
            jnp.concatenate([grad_gate, grad_up], axis=1), weight_in[...]
        )

        @pl.when(pair == last)
        def _():
            for move in moves(tile, False):
                move.start()

        return carry

    lax.fori_loop(0, tiles, tile_step, 0, unroll=True)

    slab = 512

    def weight_step(tile, carry):
        rows = pl.ds(pl.multiple_of(tile * slab, slab), slab)
        stage[rows, : 2 * width] = dot_nn(rows_turned_ref[rows, :], grad_hidden[...]).astype(
            jnp.bfloat16
        )
        stage[rows, 2 * width :] = dot_nn(grad_turned_ref[rows, :], hidden_rows[...]).astype(
            jnp.bfloat16
        )
        return carry

    lax.fori_loop(0, rows_turned_ref.shape[0] // slab, weight_step, 0)

    for number, ref in enumerate(out_refs):
        for block in range(ref.shape[0]):
            where = place(number, block)
            for which in range(2):
                for kind in range(3):
                    start = kind * width + which * units
                    ref[block, which, kind] = stage[where, start : start + units]

    @pl.when(pair == last)
    def _():
        for tile in range(tiles):
            for move in moves(tile, False):
                move.wait()


def expert_pass(
    places, steps, weights, rows, rows_turned, grads, grads_turned, gates, totals, base_expert, earlier=()
):
    first = totals is None
    token_count, model_width = rows.shape
    experts, _, depth, units = weights[0].shape[1:]

    def whole(array):
        return pl.BlockSpec(
            array.shape, lambda *_: (0,) * array.ndim, pipeline_mode=pl.Buffered(1)
        )

    weight_specs = [
        pl.BlockSpec((piece.shape[0], 2, 3, depth, units), lambda pair, _: (0, pair, 0, 0, 0))
        for piece in weights
    ]
    operands = [*weights, rows, rows_turned, grads, grads_turned, gates]
    specs = [*weight_specs, *(whole(array) for array in operands[len(weights) :])]
    aliases = {}
    if not first:
        aliases = {1 + len(operands): 0, 2 + len(operands): 1}
        operands += list(totals)
        specs += [pl.BlockSpec(memory_space=pl.ANY)] * 2
    for number, array in enumerate(earlier):
        aliases[1 + len(operands)] = 3 + len(weights) + number
        operands.append(array)
        specs.append(pl.BlockSpec(memory_space=pl.ANY))
    total_shape = jax.ShapeDtypeStruct((token_count, model_width), jnp.float32)
    products = 2 * token_count * model_width * units * experts
    return pl.pallas_call(
        functools.partial(expert_kernel, first, steps, base_expert, len(earlier)),
        grid_spec=pltpu.PrefetchScalarGridSpec(
            num_scalar_prefetch=1,
            grid=(experts // 2,),
            in_specs=specs,
            out_specs=[
                pl.BlockSpec(memory_space=pl.ANY),
                pl.BlockSpec(memory_space=pl.ANY),
                pl.BlockSpec((token_count, LANES), lambda *_: (0, 0)),
                *weight_specs,
                *([pl.BlockSpec(memory_space=pl.ANY)] * len(earlier)),
            ],
            scratch_shapes=[
                pltpu.VMEM((token_count, model_width), jnp.float32),
                pltpu.VMEM((token_count, model_width), jnp.float32),
                pltpu.VMEM((model_width, 4 * units), jnp.bfloat16),
                pltpu.VMEM((model_width, 2 * units), jnp.bfloat16),
                pltpu.VMEM((token_count, 2 * units), jnp.bfloat16),
                pltpu.VMEM((token_count, 4 * units), jnp.bfloat16),
                pltpu.VMEM((model_width, 6 * units), jnp.bfloat16),
                pltpu.SemaphoreType.DMA((4, token_count // TILE)),
            ],
        ),
        out_shape=[
            total_shape,
            total_shape,
            jax.ShapeDtypeStruct((token_count, LANES), jnp.float32),
            *(jax.ShapeDtypeStruct(piece.shape, jnp.bfloat16) for piece in weights),
            *(jax.ShapeDtypeStruct(array.shape, array.dtype) for array in earlier),
        ],
        input_output_aliases=aliases,
        compiler_params=pltpu.CompilerParams(
            dimension_semantics=("arbitrary",), vmem_limit_bytes=60 * 2**20
        ),
        cost_estimate=pl.CostEstimate(
            flops=9 * products,
            bytes_accessed=40 * 2**20,
            transcendentals=token_count * units * experts,
        ),
    )(places, *operands)


def visible_mask(first_row, first_key, row_count, key_count):
    rows = first_row + lax.broadcasted_iota(jnp.int32, (row_count, key_count), 0)
    keys = first_key + lax.broadcasted_iota(jnp.int32, (row_count, key_count), 1)
    return rows >= keys


def attend_kernel(block, heads_ref, out_ref, log_ref):
    length = heads_ref.shape[1]
    keys = heads_ref[0, :, 2 * HEAD : 3 * HEAD]
    values = heads_ref[0, :, 3 * HEAD :]
    for offset in range(0, length, block):
        limit = offset + block
        mask = visible_mask(offset, 0, block, limit)
        for which in range(2):
            lanes = slice(which * HEAD, (which + 1) * HEAD)
            query = heads_ref[0, offset:limit, lanes]
            scores = times_transposed(query, keys[:limit]) * HEAD ** (-0.5)
            scores = jnp.where(mask, scores, NEG)
            top_score = jnp.max(scores, axis=1, keepdims=True)
            exponent = jnp.exp(scores - top_score)
            denominator = jnp.sum(exponent, axis=1, keepdims=True)
            weights = (exponent * (1.0 / denominator)).astype(jnp.bfloat16)
            out_ref[0, offset:limit, lanes] = dot_nn(weights, values[:limit]).astype(jnp.bfloat16)
            log_ref[0, 0, offset:limit, which : which + 1] = top_score + jnp.log(denominator)


def attend_back_kernel(block, heads_ref, grad_ref, log_ref, out_ref, grad_keys, grad_values):
    length = heads_ref.shape[1]
    grad_keys[...] = jnp.zeros_like(grad_keys)
    grad_values[...] = jnp.zeros_like(grad_values)
    keys = heads_ref[0, :, 2 * HEAD : 3 * HEAD]
    values = heads_ref[0, :, 3 * HEAD :]
    for offset in range(0, length, block):
        limit = offset + block
        mask = visible_mask(offset, 0, block, limit)
        for which in range(2):
            lanes = slice(which * HEAD, (which + 1) * HEAD)
            query = heads_ref[0, offset:limit, lanes]
            grad = grad_ref[0, offset:limit, lanes]
            scores = times_transposed(query, keys[:limit]) * HEAD ** (-0.5)
            log_total = log_ref[0, 0, offset:limit, which : which + 1]
            weights = jnp.where(mask, jnp.exp(jnp.where(mask, scores, NEG) - log_total), 0.0)
            grad_weights = times_transposed(grad, values[:limit])
            middle = jnp.sum(weights * grad_weights, axis=1, keepdims=True)
            grad_scores = (weights * (grad_weights - middle)).astype(jnp.bfloat16)
            grad_values[:limit, :] += transposed_times(weights.astype(jnp.bfloat16), grad)
            grad_keys[:limit, :] += transposed_times(grad_scores, query)
            out_ref[0, offset:limit, lanes] = (
                dot_nn(grad_scores, keys[:limit]) * HEAD ** (-0.5)
            ).astype(jnp.bfloat16)
    out_ref[0, :, 2 * HEAD : 3 * HEAD] = (grad_keys[...] * HEAD ** (-0.5)).astype(jnp.bfloat16)
    out_ref[0, :, 3 * HEAD :] = grad_values[...].astype(jnp.bfloat16)


def attend(head_rows, grad_rows=None, log_totals=None):
    sequences, length, width = head_rows.shape
    groups = width // (4 * HEAD)
    block = min(256, length)

    def per_group(lane_count):
        return pl.BlockSpec((1, length, lane_count), lambda s, g: (s, 0, g))

    logs = pl.BlockSpec((1, 1, length, 2), lambda s, g: (s, g, 0, 0))
    work = sequences * groups * length * length * HEAD * 2
    params = pltpu.CompilerParams(
        dimension_semantics=("arbitrary", "arbitrary"), vmem_limit_bytes=48 * 2**20
    )
    if grad_rows is None:
        return pl.pallas_call(
            functools.partial(attend_kernel, block),
            grid=(sequences, groups),
            in_specs=[per_group(4 * HEAD)],
            out_specs=[per_group(2 * HEAD), logs],
            out_shape=[
                jax.ShapeDtypeStruct((sequences, length, groups * 2 * HEAD), jnp.bfloat16),
                jax.ShapeDtypeStruct((sequences, groups, length, 2), jnp.float32),
            ],
            compiler_params=params,
            cost_estimate=pl.CostEstimate(
                flops=16 * work, bytes_accessed=8 * 2**20, transcendentals=work // HEAD
            ),
        )(head_rows)
    return pl.pallas_call(
        functools.partial(attend_back_kernel, block),
        grid=(sequences, groups),
        in_specs=[per_group(4 * HEAD), per_group(2 * HEAD), logs],
        out_specs=per_group(4 * HEAD),
        out_shape=jax.ShapeDtypeStruct((sequences, length, width), jnp.bfloat16),
        scratch_shapes=[
            pltpu.VMEM((length, HEAD), jnp.float32),
            pltpu.VMEM((length, HEAD), jnp.float32),
        ],
        compiler_params=params,
        cost_estimate=pl.CostEstimate(
            flops=36 * work, bytes_accessed=8 * 2**20, transcendentals=work // HEAD
        ),
    )(head_rows, grad_rows, log_totals)


def swap_pairs(count, bit):
    return [(index, index ^ bit) for index in range(count)]


def gather_group(rows):
    count = lax.axis_size("tp")
    across = lax.ppermute(rows, "tp", swap_pairs(count, 2))
    beside = lax.ppermute(rows, "tp", swap_pairs(count, 1))
    corner = lax.ppermute(across, "tp", swap_pairs(count, 1))
    return jnp.concatenate([rows, beside, across, corner], axis=0)


def scatter_group(terms):
    count = lax.axis_size("tp")
    parts = terms.reshape(count, -1, terms.shape[-1])
    first, second = (
        lax.ppermute(parts[which].astype(jnp.bfloat16), "tp", swap_pairs(count, 1)).astype(
            jnp.float32
        )
        for which in (3, 1)
    )
    passed = lax.ppermute((parts[2] + first).astype(jnp.bfloat16), "tp", swap_pairs(count, 2))
    return parts[0] + second + passed.astype(jnp.float32)


def shifted(count, step):
    return [(index, (index + step) % count) for index in range(count)]


def gather_axis(piece, name):
    count = lax.axis_size(name)
    mine = lax.axis_index(name)
    found = [piece] + [
        lax.ppermute(piece, name, shifted(count, -step)) for step in range(1, count)
    ]
    return lax.dynamic_slice_in_dim(
        jnp.stack(found + found[:-1]), (count - mine) % count, count, axis=0
    )


def gather_bit(piece, bit):
    other = lax.ppermute(piece, "tp", swap_pairs(lax.axis_size("tp"), bit))
    upper = (lax.axis_index("tp") & bit) > 0
    return jnp.where(upper, jnp.stack([other, piece]), jnp.stack([piece, other]))


def gather_dense(piece):
    fsdp_count, context_count = lax.axis_size("fsdp"), lax.axis_size("ctx")
    whole = gather_bit(gather_bit(gather_axis(gather_axis(piece, "fsdp"), "ctx"), 2), 1)
    whole = whole.reshape((2, 2, context_count, fsdp_count) + piece.shape)
    return whole.transpose(3, 2, 1, 0, 4, 5).reshape((-1,) + piece.shape)


def scatter_axis(parts, name):
    count = lax.axis_size(name)
    mine = lax.axis_index(name)
    low = parts.astype(jnp.bfloat16)
    total = lax.dynamic_index_in_dim(parts, mine, 0, keepdims=False).astype(jnp.float32)
    for step in range(1, count):
        sent = lax.dynamic_index_in_dim(low, (mine + step) % count, 0, keepdims=False)
        total = total + lax.ppermute(sent, name, shifted(count, step)).astype(jnp.float32)
    return total


def scatter_bit(parts, bit, axis):
    mine = (lax.axis_index("tp") & bit) // bit
    sent = lax.dynamic_index_in_dim(parts, 1 - mine, axis, keepdims=False).astype(jnp.bfloat16)
    kept = lax.dynamic_index_in_dim(parts, mine, axis, keepdims=False).astype(jnp.float32)
    return kept + lax.ppermute(sent, "tp", swap_pairs(lax.axis_size("tp"), bit)).astype(
        jnp.float32
    )


def scatter_dense(parts):
    fsdp_count, context_count = lax.axis_size("fsdp"), lax.axis_size("ctx")
    parts = parts.reshape((fsdp_count, context_count, 2, 2) + parts.shape[1:])
    parts = scatter_bit(scatter_bit(parts, 1, 3), 2, 2)
    return scatter_axis(scatter_axis(jnp.moveaxis(parts, 1, 0), "ctx"), "fsdp")


def hold(*refs):
    pass


def together(*values):
    spec = pl.BlockSpec(memory_space=pl.ANY)
    return pl.pallas_call(
        hold,
        in_specs=[spec] * len(values),
        out_specs=[spec] * len(values),
        out_shape=[jax.ShapeDtypeStruct(value.shape, value.dtype) for value in values],
        input_output_aliases={number: number for number in range(len(values))},
    )(*values)


def after(value, *earlier):
    spec = pl.BlockSpec(memory_space=pl.ANY)
    return pl.pallas_call(
        hold,
        in_specs=[spec] * (1 + len(earlier)),
        out_specs=spec,
        out_shape=jax.ShapeDtypeStruct(value.shape, value.dtype),
        input_output_aliases={0: 0},
    )(value, *earlier)


def per_device(
    tokens,
    routes,
    cotangent,
    norm_gains,
    query_key_value,
    attn_output,
    router_weight,
    expert_in,
    expert_out,
):
    local_seqs, local_positions, model_width = tokens.shape
    context_count = lax.axis_size("ctx")
    length = local_positions * context_count
    row_count = local_seqs * local_positions
    local_groups = KV_HEADS // context_count
    head_size = HEAD
    score_scale = HEAD ** (-0.5)
    capacity = local_positions * 3 // 8
    group_grads = by_rows(gather_group(cotangent.reshape(row_count, model_width)))
    grads_turned = by_rows(group_grads.T)
    device_count = context_count * lax.axis_size("fsdp") * lax.axis_size("tp")
    gain_count, router_count = norm_gains.size, router_weight.size
    packed = lax.all_gather(pack_rows([query_key_value, norm_gains], model_width), ALL_AXES, axis=0)
    shard_depth = expert_in.shape[2]
    chunk_experts = EXPERTS // CHUNKS
    paired = context_count == 2
    expert_shards = jnp.concatenate([expert_in, expert_out[:, None]], axis=1)
    if paired:
        last_other = lax.ppermute(
            expert_shards[EXPERTS - chunk_experts :], "ctx", swap_pairs(2, 1)
        )
        packed, last_other = together(after(packed, grads_turned), last_other)
    else:
        packed = after(packed, grads_turned)
    packed_later = gather_dense(pack_rows([attn_output, router_weight], model_width))
    inward_rows, output_rows = query_key_value.shape[0], attn_output.shape[0]
    inward_full = packed[:, :inward_rows].reshape(-1, model_width)
    gain_full = (
        packed[:, inward_rows:]
        .reshape(device_count, -1)[:, :gain_count]
        .reshape(device_count, 2, -1)
        .transpose(1, 0, 2)
        .reshape(2, model_width)
    )
    output_full = packed_later[:, :output_rows].reshape(-1, model_width)
    router_full = (
        packed_later[:, output_rows:]
        .reshape(device_count, -1)[:, :router_count]
        .reshape(device_count, EXPERTS, -1)
        .transpose(1, 0, 2)
        .reshape(EXPERTS, model_width)
    )
    my_context = lax.axis_index("ctx").astype(jnp.int32)
    if paired:
        places = jnp.stack([my_context, 1 - my_context]) * shard_depth
        steps = (2 * shard_depth, 2 * shard_depth)
    else:
        places = jnp.zeros((1,), jnp.int32)
        steps = (shard_depth,)
    expert_pieces = []
    for chunk in range(CHUNKS):
        shard = expert_shards[chunk * chunk_experts : (chunk + 1) * chunk_experts]
        if paired:
            expert_pieces.append([lax.all_gather(shard, "fsdp", axis=0)])
            if chunk == CHUNKS - 1:
                expert_pieces[chunk].append(lax.all_gather(last_other, "fsdp", axis=0))
        else:
            expert_pieces.append([lax.all_gather(shard, ("fsdp", "ctx"), axis=0)])
    gain_rows = gain_full.astype(jnp.float32)
    inputs = tokens.astype(jnp.float32).reshape(row_count, model_width)
    inverse_first = lax.rsqrt(jnp.mean(inputs * inputs, axis=1, keepdims=True) + EPS)
    normed_first = inputs * inverse_first
    first_low = (normed_first * gain_rows[0]).astype(jnp.bfloat16)
    projected = times_transposed(first_low, inward_full).reshape(
        local_seqs, local_positions, KV_HEADS, 4, head_size
    )
    positions = lax.axis_index("ctx") * local_positions + jnp.arange(
        local_positions, dtype=jnp.int32
    )
    cosine_table, sine_table = angle_tables(positions, head_size)
    cosine_rows = cosine_table[None, :, None, None, :]
    sine_rows = sine_table[None, :, None, None, :]
    turned = jnp.concatenate(
        [rotary(projected[:, :, :, :3], cosine_rows, sine_rows), projected[:, :, :, 3:]], axis=3
    )
    sent_heads = turned.astype(jnp.bfloat16).reshape(
        local_seqs, local_positions, KV_HEADS, 4 * head_size
    )
    head_rows = lax.all_to_all(sent_heads, "ctx", split_axis=2, concat_axis=1, tiled=True)
    head_rows = head_rows.reshape(local_seqs, length, -1)
    head_output, log_totals = attend(head_rows)
    head_output = head_output.reshape(local_seqs, length, local_groups, 2 * head_size)
    merged = lax.all_to_all(head_output, "ctx", split_axis=1, concat_axis=2, tiled=True).reshape(
        row_count, HEADS * head_size
    )
    hidden = inputs + times_transposed(merged, output_full)
    inverse_second = lax.rsqrt(jnp.mean(hidden * hidden, axis=1, keepdims=True) + EPS)
    normed_second = hidden * inverse_second
    second_low = (normed_second * gain_rows[1]).astype(jnp.bfloat16)
    group_rows = by_rows(gather_group(by_rows(second_low)))
    group_count = group_rows.shape[0]
    chances = jax.nn.softmax(times_transposed(group_rows, router_full), axis=-1)
    group_order = jnp.bitwise_xor(
        jnp.arange(lax.axis_size("tp"), dtype=jnp.int32), lax.axis_index("tp").astype(jnp.int32)
    )
    route_rows = jnp.take(
        routes.reshape(lax.axis_size("tp"), row_count, TOP), group_order, axis=0
    ).reshape(group_count, TOP)
    chosen_any = jnp.sum(
        (route_rows[:, :, None] == jnp.arange(EXPERTS, dtype=jnp.int32)[None, None, :]).astype(
            jnp.float32
        ),
        axis=1,
    )
    gates = jnp.pad(chances * chosen_any, ((0, 0), (0, LANES - EXPERTS)))
    group_turned = by_rows(group_rows.T)
    totals = None
    choice_total = None
    chunk_sums = []
    own_sums = []
    far_sums = []
    arrivals = []
    marks = []

    def fetch(chunk):
        near = expert_pieces[chunk][0]
        if chunk > 1:
            near = after(near, marks[chunk - 2])
            expert_pieces[chunk][0] = near
        expert_pieces[chunk].append(lax.ppermute(near, "ctx", swap_pairs(2, 1)))

    def cross(chunk):
        arrivals.append(lax.ppermute(far_sums[chunk], "ctx", swap_pairs(2, 1)))

    if paired:
        fetch(0)
    for chunk in range(CHUNKS):
        if paired:
            if chunk + 2 < CHUNKS:
                fetch(chunk + 1)
        moe_total, back_total, choice, *grad_pieces = expert_pass(
            places,
            steps,
            expert_pieces[chunk],
            group_rows,
            group_turned,
            group_grads,
            grads_turned,
            gates,
            totals,
            chunk * chunk_experts,
            arrivals if paired and chunk == CHUNKS - 1 else (),
        )
        totals = (moe_total, back_total)
        marks.append(choice)
        choice_total = choice if choice_total is None else choice_total + choice
        if paired:
            own_sums.append(grad_pieces[0])
            far_sums.append(grad_pieces[1])
            if chunk == 1:
                cross(1)
            elif chunk == CHUNKS - 1:
                arrivals[0] = grad_pieces[2]
        else:
            chunk_sums.append(
                lax.psum_scatter(grad_pieces[0], ("fsdp", "ctx"), scatter_dimension=0)
            )
    if paired:
        cross(2)
        first_sums = [
            by_rows(lax.psum_scatter(part, "fsdp", scatter_dimension=0))
            for part in (far_sums[0], own_sums[0])
        ]
    grad_chances = choice_total[:, :EXPERTS] * chosen_any
    grad_logits = chances * (grad_chances - jnp.sum(grad_chances * chances, axis=-1, keepdims=True))
    router_rows = router_full.astype(jnp.float32)
    grad_router = jnp.dot(grad_logits.T, group_rows.astype(jnp.float32), precision=HIGH)
    back_group = by_rows(totals[1] + jnp.dot(grad_logits, router_rows, precision=HIGH))
    if paired:
        back_group, *held = together(
            back_group, *first_sums, *arrivals, far_sums[-1], own_sums[-1]
        )
        first_sums, arrivals = held[:2], held[2:4]
        last_sums = [
            by_rows(lax.psum_scatter(part, "fsdp", scatter_dimension=0)) for part in held[4:]
        ]
    grad_second = by_rows(scatter_group(back_group))
    grad_gain_second = jnp.sum(grad_second * normed_second, axis=0)
    grad_hidden = cotangent.astype(jnp.float32).reshape(row_count, model_width) + rms_back(
        grad_second, normed_second, inverse_second, gain_rows[1]
    )
    grad_attn = by_rows(grad_hidden.astype(jnp.bfloat16))
    moe_rows = by_rows(scatter_group(after(totals[0], grad_attn)))
    output = (hidden + moe_rows).astype(jnp.bfloat16).reshape(tokens.shape)
    grad_output_weight = transposed_times(grad_attn, merged)
    grad_merged = (
        jnp.dot(grad_attn, output_full, preferred_element_type=jnp.float32)
        .astype(jnp.bfloat16)
        .reshape(local_seqs, local_positions, KV_HEADS, 2 * head_size)
    )
    grad_heads = lax.all_to_all(by_rows(grad_merged), "ctx", split_axis=2, concat_axis=1, tiled=True)
    grad_head_rows = attend(
        head_rows, grad_heads.reshape(local_seqs, length, -1), log_totals
    ).reshape(local_seqs, length, local_groups, 4 * head_size)
    grad_turned = (
        lax.all_to_all(grad_head_rows, "ctx", split_axis=1, concat_axis=2, tiled=True)
        .astype(jnp.float32)
        .reshape(local_seqs, local_positions, KV_HEADS, 4, head_size)
    )
    grad_projected = (
        jnp.concatenate(
            [
                rotary_back(grad_turned[:, :, :, :3], cosine_rows, sine_rows),
                grad_turned[:, :, :, 3:],
            ],
            axis=3,
        )
        .astype(jnp.bfloat16)
        .reshape(row_count, -1)
    )
    if paired:
        for own, arrived in zip(own_sums[1:-1], arrivals):
            joined = (own.astype(jnp.float32) + arrived.astype(jnp.float32)).astype(jnp.bfloat16)
            chunk_sums.append(lax.psum_scatter(joined, "fsdp", scatter_dimension=0))
        first_sums[0] = after(first_sums[0], grad_projected)
        for far, own in (first_sums, last_sums):
            far = lax.ppermute(far, "ctx", swap_pairs(2, 1))
            chunk_sums.append(own.astype(jnp.float32) + far.astype(jnp.float32))
        chunk_sums = [chunk_sums[2], chunk_sums[0], chunk_sums[1], chunk_sums[3]]
    grad_inward = transposed_times(grad_projected, first_low)
    grad_first = jnp.dot(grad_projected, inward_full, preferred_element_type=jnp.float32)
    grad_gain_first = jnp.sum(grad_first * normed_first, axis=0)
    grad_inputs = grad_hidden + rms_back(grad_first, normed_first, inverse_first, gain_rows[0])
    grad_gains = jnp.stack([grad_gain_first, grad_gain_second])

    def by_device(array, axis):
        parts = array.reshape(
            array.shape[:axis] + (device_count, -1) + array.shape[axis + 1 :]
        )
        return jnp.moveaxis(parts, axis, 0).reshape(device_count, -1)

    inward_sum = scatter_dense(
        grad_inward.astype(jnp.bfloat16).reshape((device_count,) + query_key_value.shape)
    )
    output_sum = scatter_dense(
        grad_output_weight.astype(jnp.bfloat16).reshape((device_count,) + attn_output.shape)
    )
    small = jnp.concatenate([by_device(grad_router, 1), by_device(grad_gains, 1)], axis=1)
    small_count = small.shape[1]
    small_rows = -(-small_count // (16 * LANES)) * 16
    small = jnp.pad(small, ((0, 0), (0, small_rows * LANES - small_count)))
    small_sum = scatter_dense(small.reshape(device_count, small_rows, LANES)).reshape(-1)
    return (
        output,
        grad_inputs.reshape(tokens.shape),
        small_sum[router_count:small_count].reshape(norm_gains.shape),
        inward_sum,
        output_sum,
        small_sum[:router_count].reshape(router_weight.shape),
        jnp.concatenate([part[:, :2].astype(jnp.float32) for part in chunk_sums], axis=0),
        jnp.concatenate([part[:, 2].astype(jnp.float32) for part in chunk_sums], axis=0),
    )


def solution(mesh):
    placed = (
        P(("fsdp", "tp"), "ctx", None),
        P("fsdp", "ctx", None),
        P(("fsdp", "tp"), "ctx", None),
        P(None, ("fsdp", "ctx", "tp")),
        P(("fsdp", "ctx", "tp"), None),
        P(("fsdp", "ctx", "tp"), None),
        P(None, ("fsdp", "ctx", "tp")),
        P(None, None, ("fsdp", "ctx"), "tp"),
        P(None, ("fsdp", "ctx"), "tp"),
    )
    return jax.shard_map(
        per_device,
        mesh=mesh,
        in_specs=placed,
        out_specs=(
            P(("fsdp", "tp"), "ctx", None),
            P(("fsdp", "tp"), "ctx", None),
            P(None, ("fsdp", "ctx", "tp")),
            P(("fsdp", "ctx", "tp"), None),
            P(("fsdp", "ctx", "tp"), None),
            P(None, ("fsdp", "ctx", "tp")),
            P(None, None, ("fsdp", "ctx"), "tp"),
            P(None, ("fsdp", "ctx"), "tp"),
        ),
        check_vma=False,
    )
```
